128 devices in a mesh: frag: 32 (over y, z, core), aux: 4 (over x).
Axes of the slice: x: 4, y: 4, z: 4, core: 2. Of those that a mesh axis runs over, the one named last changes fastest.
Arguments:
- blocks: bfloat16 [32, 3008, 4096], P('frag', 'aux'), may hold values from -0.0546875 to 0.0546875
- occ_energy: float32 [32, 16], replicated, may hold values from -2 to -0.5
- vir_energy: float32 [32, 256], replicated, may hold values from 0.5 to 3
- occ_count: int32 [32], replicated, may hold values from 8 to 16, as said below
- vir_count: int32 [32], replicated, may hold values from 128 to 256, as said below
- partner_offset: int32 [32], P('frag'), may hold values from 1 to 3, as said below
Outputs:
- pair_energy: float32 [32], P('frag')
- density: float32 [32, 256, 256], P('frag', 'aux')
The draws below stay inside these ranges and needn't reach their ends.
Inputs may be any that keep to these rules, and one draw needn't show every extreme that they name: `occ_count`: every count lies in 8 to 16, and some fragment holds exactly 16. `vir_count`: every count lies in 128 to 256, and some fragment holds exactly 256. Padded orbitals take no part in any pair. `partner_offset`: partners are 1 to 3 fragments ahead; both ends occur in every draw. A partner at 32 or beyond means the fragment leads no pair.
All inputs are finite; a program needn't handle non-finite values.
Results may differ from the reference program's by a relative error of at most 0.0003.
Values may be sent and summed in bfloat16 or wider, within the bound.
A program may use at most 192 MiB of HBM per device.

```python
import jax
import jax.numpy as jnp
from jax import lax

OCC = 16
VIR = 256
AUX = 3008
REACH = 3
NFRAG = 32


def forced_counts(key, lowest, highest):
    draw_key, spot_key = jax.random.split(key)
    values = jax.random.randint(draw_key, (NFRAG,), lowest, highest + 1, dtype=jnp.int32)
    spot = jax.random.randint(spot_key, (), 0, NFRAG, dtype=jnp.int32)
    return values.at[spot].set(highest)


def draw_occ_count(key, part):
    key = jax.random.fold_in(key, 11)
    return forced_counts(key, OCC // 2, OCC)


def draw_vir_count(key, part):
    key = jax.random.fold_in(key, 23)
    return forced_counts(key, VIR // 2, VIR)


def draw_partner_offset(key, part):
    key = jax.random.fold_in(key, 37)
    draw_key, spot_key = jax.random.split(key)
    values = jax.random.randint(draw_key, (NFRAG,), 1, REACH + 1, dtype=jnp.int32)
    spot = jax.random.randint(spot_key, (), 0, NFRAG, dtype=jnp.int32)
    values = values.at[spot].set(REACH)
    return values.at[(spot + 1) % NFRAG].set(1)


def level_of(own_key, shape, cuts, smallest, top_value):
    factor_of, own = 1.0, jax.random.fold_in(own_key, 6)
    for dim, shards_of in cuts:
        heights = jnp.exp(jax.random.uniform(jax.random.fold_in(own, dim), (shards_of,), jnp.float32, smallest / len(cuts), top_value / len(cuts)))
        factor_of = factor_of * jnp.repeat(heights, shape[dim] // shards_of).reshape([-1 if axis == dim else 1 for axis in range(len(shape))])
    return factor_of


def scatter_about(key, extent, scale, most, cuts=(), kind=jnp.bfloat16):
    result = scale * jax.random.normal(key, extent, jnp.float32)
    if cuts:
        result = result * level_of(key, extent, cuts, -0.22, 0.18)
    return jnp.clip(result, -most, most).astype(kind)


def setup_inputs(seed: int = 0) -> dict:
    streams_of = jax.random.split(jax.random.key(seed), 7)
    return {
        "blocks": scatter_about(streams_of[0], (NFRAG, AUX, OCC * VIR), (50 * VIR) ** -0.5, 0.0546875, ((0, 32), (1, 4))),
        "occ_energy": jnp.clip(jax.random.uniform(streams_of[1], (NFRAG, OCC), jnp.float32, -2.0, -0.5), -2.0, -0.5),
        "vir_energy": jnp.clip(jax.random.uniform(streams_of[2], (NFRAG, VIR), jnp.float32, 0.5, 3.0), 0.5, 3.0),
        "occ_count": draw_occ_count(jax.random.fold_in(streams_of[6], 71), 0),
        "vir_count": draw_vir_count(jax.random.fold_in(streams_of[6], 71), 0),
        "partner_offset": draw_partner_offset(jax.random.fold_in(streams_of[6], 71), 0),
    }


def pair_terms(fragment, blocks, occ_energy, vir_energy, occ_count, vir_count, partner_offset):
    frag_total = blocks.shape[0]
    partner = fragment + partner_offset[fragment]
    valid = partner < frag_total
    clipped = jnp.minimum(partner, frag_total - 1).astype(jnp.int32)
    first_block = blocks[fragment]
    second_block = blocks[clipped]
    integrals = lax.dot_general(first_block, second_block, (((0,), (0,)), ((), ())), preferred_element_type=jnp.float32)
    occ_ids = jnp.arange(OCC, dtype=jnp.int32)
    vir_ids = jnp.arange(VIR, dtype=jnp.int32)
    row_energy = (occ_energy[fragment][:, None] - vir_energy[fragment][None, :]).reshape(OCC * VIR)
    col_energy = (occ_energy[clipped][:, None] - vir_energy[clipped][None, :]).reshape(OCC * VIR)
    row_mask = ((occ_ids < occ_count[fragment])[:, None] & (vir_ids < vir_count[fragment])[None, :]).reshape(OCC * VIR)
    col_mask = ((occ_ids < occ_count[clipped])[:, None] & (vir_ids < vir_count[clipped])[None, :]).reshape(OCC * VIR)
    full_mask = row_mask[:, None] & col_mask[None, :] & valid
    amplitude = jnp.where(full_mask, integrals / (row_energy[:, None] + col_energy[None, :]), jnp.float32(0.0))
    energy = jnp.sum(amplitude * integrals)
    amp_half = amplitude.astype(jnp.bfloat16)
    by_virtual = amp_half.reshape(OCC, VIR, OCC * VIR).transpose(1, 0, 2).reshape(VIR, OCC * OCC * VIR)
    first_part = jnp.dot(by_virtual, by_virtual.T, preferred_element_type=jnp.float32)
    by_column = amp_half.reshape(OCC * VIR * OCC, VIR)
    second_part = jnp.dot(by_column.T, by_column, preferred_element_type=jnp.float32)
    return energy, first_part, second_part, clipped


def reference(blocks, occ_energy, vir_energy, occ_count, vir_count, partner_offset):
    frag_total = blocks.shape[0]

    def one_pair(fragment):
        return pair_terms(fragment, blocks, occ_energy, vir_energy, occ_count, vir_count, partner_offset)

    energies, first_parts, second_parts, partners = lax.map(one_pair, jnp.arange(frag_total, dtype=jnp.int32))
    density = first_parts + jnp.zeros_like(first_parts).at[partners].add(second_parts)
    return energies, density
```

```python
import functools

import jax
import jax.numpy as jnp
from jax import lax
from jax.experimental import pallas as pl
from jax.experimental.pallas import tpu as pltpu
from jax.sharding import PartitionSpec as P

LEAD = 2
PIECES = 4
BLOCK = 256


def pieces_of(rows):
    step = -(-rows // (16 * PIECES)) * 16
    return [(at, min(step, rows - at)) for at in range(0, rows, step)]


def to_device(src, dst, send_sem, recv_sem, frag, aux):
    return pltpu.make_async_remote_copy(
        src_ref=src,
        dst_ref=dst,
        send_sem=send_sem,
        recv_sem=recv_sem,
        device_id={"frag": frag, "aux": aux},
        device_id_type=pl.DeviceIdType.MESH,
    )


def kernel(
    frag_total,
    blocks,
    occ_energy,
    vir_energy,
    occ_count,
    vir_count,
    offset,
    energy_out,
    density_out,
    a_half,
    a_other,
    b_half,
    b_other,
    cand,
    b_turned,
    base,
    keep,
    total,
    landed,
    summed,
    parts,
    off_send,
    off_here,
    off_scalar,
    a_in,
    a_up,
    a_send,
    a_recv,
    cand_send,
    cand_recv,
    cand_pass,
    b_send,
    b_recv,
    off_sems,
    sum_send,
    sum_recv,
    part_send,
    part_recv,
):
    rows = blocks.shape[1]
    half = blocks.shape[2] // 2
    vir = vir_energy.shape[1]
    steps = b_half.shape[0]
    pieces = pieces_of(rows)
    padded = a_half.shape[0]
    aux_rows = vir // 4
    chips = frag_total // 2

    frag = lax.axis_index("frag")
    aux = lax.axis_index("aux")
    core = lax.rem(frag, 2)
    chip = frag // 2
    up = lax.rem(chip + 1, chips)
    down = lax.rem(chip + chips - 1, chips)
    sibling = chip * 2 + 1 - core

    near = aux + 1 - 2 * lax.rem(aux, 2)
    side = 3 - aux
    far = lax.rem(aux + 2, 4)
    by_near = aux // 2
    by_side = lax.rem((aux + 1) // 2, 2)
    a_mate = jnp.where(core == 0, near, side)
    b_mate = jnp.where(core == 0, side, near)
    p_half = jnp.where(core == 0, by_near, by_side)
    q_half = jnp.where(core == 0, by_side, by_near)

    barrier = pltpu.get_barrier_semaphore()
    for other in (near, side, far):
        pl.semaphore_signal(
            barrier, inc=1, device_id={"frag": frag, "aux": other}, device_id_type=pl.DeviceIdType.MESH
        )
    for other in (sibling, up * 2, up * 2 + 1, down * 2, down * 2 + 1):
        pl.semaphore_signal(
            barrier, inc=1, device_id={"frag": other, "aux": aux}, device_id_type=pl.DeviceIdType.MESH
        )
    pl.semaphore_wait(barrier, 8)

    p_cols = pl.ds(pl.multiple_of(p_half * half, 256), half)
    p_rest = pl.ds(pl.multiple_of((1 - p_half) * half, 256), half)

    def own_rows(who, at, size):
        return pl.ds(pl.multiple_of(who * rows + at, 16), size)

    def a_first(n, at, size, there):
        src = blocks.at[0, pl.ds(at, size), p_cols]
        dst = a_half.at[own_rows(aux, at, size)]
        if there is None:
            return pltpu.make_async_copy(src, dst, a_in.at[0, n])
        return to_device(src, dst, a_up.at[0, n], a_in.at[0, n], there, aux)

    def a_second(n, at, size, there):
        src = blocks.at[0, pl.ds(at, size), p_rest]
        dst = a_other.at[pl.ds(at, size)]
        if there is None:
            return pltpu.make_async_copy(src, dst, a_in.at[1, n])
        return to_device(src, dst, a_up.at[1, n], a_in.at[1, n], there, aux)

    def off_copy():
        return to_device(off_send, off_here, off_sems.at[0], off_sems.at[1], up * 2 + 1, aux)

    def cand_copy(j, slot, n, there):
        src = blocks.at[0, :, pl.ds(pl.multiple_of(j * 2 * vir, 256), 2 * vir)]
        if there is None:
            return pltpu.make_async_copy(src, cand.at[slot, j], cand_recv.at[slot, j])
        return to_device(src, cand.at[slot, j], cand_send.at[n, j], cand_recv.at[slot, j], there, aux)

    def cand_forward(j):
        return to_device(cand.at[2, j], cand.at[1, j], cand_pass.at[j], cand_recv.at[1, j], sibling, aux)

    off_send[...] = jnp.full(off_send.shape, offset[0], jnp.int32)

    @pl.when(core == 0)
    def _():
        for n, (at, size) in enumerate(pieces):
            a_first(n, at, size, None).start()
            a_second(n, at, size, None).start()

        @pl.loop(0, steps)
        def _(j):
            cand_copy(j, 2, 1, down * 2 + 1).start()
            cand_copy(j, 0, 0, sibling).start()

    @pl.when(core == 1)
    def _():
        off_copy().start()
        for n, (at, size) in enumerate(pieces):
            a_first(n, at, size, up * 2 + 1).start()
            a_second(n, at, size, up * 2 + 1).start()

        @pl.loop(0, steps)
        def _(j):
            cand_copy(j, 2, 1, down * 2).start()
            cand_copy(j, 0, 0, sibling).start()
            cand_copy(j, 1, 0, None).start()

    def a_direct(n, at, size):
        here = a_half.at[own_rows(aux, at, size)]
        return to_device(here, here, a_send.at[0, n], a_recv.at[0, n], frag, a_mate)

    def a_across(n, at, size):
        return to_device(
            a_other.at[pl.ds(at, size)],
            a_half.at[own_rows(aux, at, size)],
            a_send.at[1, n],
            a_recv.at[1, n],
            frag,
            b_mate,
        )

    def a_forward(n, at, size):
        here = a_half.at[own_rows(b_mate, at, size)]
        return to_device(here, here, a_send.at[2, n], a_recv.at[2, n], frag, a_mate)

    def a_landing(kind, who, n, at, size):
        here = a_half.at[own_rows(who, at, size)]
        return to_device(here, here, a_send.at[kind, n], a_recv.at[kind, n], frag, a_mate)

    if padded > 4 * rows:
        a_half[4 * rows :, :] = jnp.zeros((padded - 4 * rows, half), jnp.bfloat16)

        @pl.loop(0, steps)
        def _(j):
            b_half[j, 4 * rows :, :] = jnp.zeros((padded - 4 * rows, vir), jnp.bfloat16)

    for n, (at, size) in enumerate(pieces):
        @pl.when(core == 0)
        def _():
            a_first(n, at, size, None).wait()
            a_second(n, at, size, None).wait()

        @pl.when(core == 1)
        def _():
            a_first(n, at, size, up * 2 + 1).wait_recv()
            a_second(n, at, size, up * 2 + 1).wait_recv()

        a_across(n, at, size).start()
        a_direct(n, at, size).start()

    @pl.when(core == 0)
    def _():
        off_here[...] = off_send[...]

    @pl.when(core == 1)
    def _():
        off_copy().wait()

    scalar_copy = pltpu.make_async_copy(off_here, off_scalar, off_sems.at[2])
    scalar_copy.start()
    scalar_copy.wait()
    distance = off_scalar[0, 0]
    leader = jnp.where(core == 0, frag, lax.rem(chip * 2 + frag_total - 1, frag_total))
    partner = jnp.minimum(leader + distance, frag_total - 1)
    valid = leader + distance < frag_total
    leader_occ = occ_count[leader]
    partner_occ = occ_count[partner]
    leader_vir = vir_count[leader]
    partner_vir = vir_count[partner]

    row_levels = jnp.broadcast_to(vir_energy[pl.ds(partner, 1), :], (vir, vir)).T
    base[...] = -vir_energy[pl.ds(leader, 1), :] - row_levels
    row_ids = lax.broadcasted_iota(jnp.int32, (vir, vir), 0)
    col_ids = lax.broadcasted_iota(jnp.int32, (vir, vir), 1)
    keep[...] = jnp.where((row_ids < partner_vir) & (col_ids < leader_vir), 1.0, 0.0)
    total[...] = jnp.zeros(total.shape, jnp.float32)

    for n, (at, size) in enumerate(pieces):
        a_landing(1, b_mate, n, at, size).wait_recv()
        a_forward(n, at, size).start()

    def b_direct(j):
        here = b_half.at[j, own_rows(aux, 0, rows)]
        return to_device(here, here, b_send.at[0, j], b_recv.at[0, j], frag, b_mate)

    def b_across(j):
        return to_device(
            b_other.at[j],
            b_half.at[j, own_rows(aux, 0, rows)],
            b_send.at[1, j],
            b_recv.at[1, j],
            frag,
            a_mate,
        )

    def b_forward(j):
        here = b_half.at[j, own_rows(a_mate, 0, rows)]
        return to_device(here, here, b_send.at[2, j], b_recv.at[2, j], frag, b_mate)

    def b_landing(kind, who, j):
        here = b_half.at[j, own_rows(who, 0, rows)]
        return to_device(here, here, b_send.at[kind, j], b_recv.at[kind, j], frag, b_mate)

    def chosen(j, which):
        cols = pl.ds(pl.multiple_of(which * vir, 128), vir)
        one, two, three = (cand[n, j, :, cols] for n in range(3))
        return jnp.where(distance == 1, one, jnp.where(distance == 2, two, three))

    def begin(j):
        @pl.when(core == 1)
        def _():
            cand_copy(j, 2, 1, down * 2).wait_recv()
            cand_forward(j).start()
            cand_copy(j, 0, 0, sibling).wait_recv()
            cand_copy(j, 1, 0, None).wait()

        @pl.when(core == 0)
        def _():
            cand_copy(j, 0, 0, sibling).wait_recv()
            cand_copy(j, 2, 1, down * 2).wait_recv()
            cand_forward(j).wait_recv()

        b_other[j] = chosen(j, 1 - q_half)
        b_across(j).start()
        b_half[j, own_rows(aux, 0, rows), :] = chosen(j, q_half)
        b_direct(j).start()

    def pass_on(j):
        b_landing(1, a_mate, j).wait_recv()
        b_forward(j).start()

    def work(j):
        for at in range(0, padded, BLOCK):
            b_turned[:, at : at + BLOCK] = b_half[j, at : at + BLOCK, :].T
        col_occ = 2 * j + q_half
        col_level = occ_energy[partner, col_occ]
        col_ok = jnp.logical_and(valid, col_occ < partner_occ)

        def tile(i, carry):
            row_occ = p_half * steps + i
            ok = jnp.where(jnp.logical_and(col_ok, row_occ < leader_occ), 1.0, 0.0)
            level = occ_energy[leader, row_occ] + col_level
            integrals = jnp.dot(
                b_turned[...],
                a_half[:, pl.ds(pl.multiple_of(i * vir, 128), vir)],
                preferred_element_type=jnp.float32,
            )
            amplitude = integrals * (keep[...] * ok) / (base[...] + level)
            energy = amplitude * integrals
            rounded = amplitude.astype(jnp.bfloat16)
            first = lax.dot_general(
                rounded, rounded, (((0,), (0,)), ((), ())), preferred_element_type=jnp.float32
            )
            second = lax.dot_general(
                rounded, rounded, (((1,), (1,)), ((), ())), preferred_element_type=jnp.float32
            )
            for n in range(4):
                piece = slice(n * aux_rows, (n + 1) * aux_rows)
                total[n, :aux_rows, :] += first[piece]
                total[n, aux_rows : 2 * aux_rows, :] += second[piece]
            total[0, 2 * aux_rows :, :] += energy.reshape(vir // 8, 8, vir).sum(0)
            return carry

        lax.fori_loop(0, steps, tile, 0)

    for j in range(LEAD):
        begin(j)
    pass_on(0)

    for n, (at, size) in enumerate(pieces):
        a_landing(0, a_mate, n, at, size).wait_recv()
        a_landing(2, far, n, at, size).wait_recv()

    @pl.loop(0, steps)
    def _(j):
        @pl.when(j + LEAD < steps)
        def _():
            begin(j + LEAD)

        @pl.when(j + 1 < steps)
        def _():
            pass_on(j + 1)

        b_landing(0, b_mate, j).wait_recv()
        b_landing(2, far, j).wait_recv()
        work(j)

    for n in range(1, 4):
        total[n, 2 * aux_rows :, :] = total[0, 2 * aux_rows :, :]

    def sum_copy(n):
        there = lax.rem(aux + n, 4)
        return to_device(
            total.at[there], landed.at[4 - n], sum_send.at[n - 1], sum_recv.at[n - 1], frag, there
        )

    for n in (2, 1, 3):
        sum_copy(n).start()
    landed[0] = total[aux]
    for n in (1, 3, 2):
        sum_copy(n).wait()
    sums = landed[lax.rem(4 - aux, 4)]
    for n in range(1, 4):
        sums = sums + landed[lax.rem(n + 4 - aux, 4)]
    summed[0, :aux_rows, :] = sums[:aux_rows]
    summed[0, aux_rows:, :] = sums[2 * aux_rows :]
    for n in range(1, 4):
        summed[n, :aux_rows, :] = jnp.where(distance == n, sums[aux_rows : 2 * aux_rows], 0.0)

    def part_copy(n, there):
        if n == 0:
            src, dst = summed.at[0], parts.at[0]
        else:
            src, dst = summed.at[n, pl.ds(0, aux_rows)], parts.at[n, pl.ds(0, aux_rows)]
        return to_device(src, dst, part_send.at[n], part_recv.at[n], there, aux)

    @pl.when(core == 0)
    def _():
        part_copy(3, up * 2 + 1).start()
        part_copy(2, up * 2).start()
        part_copy(1, sibling).start()
        parts[0] = summed[0]
        for n in (1, 2, 3):
            part_copy(n, sibling).wait()

    @pl.when(core == 1)
    def _():
        part_copy(0, down * 2 + 1).start()
        part_copy(3, up * 2).start()
        part_copy(1, sibling).start()
        parts[2, :aux_rows, :] = summed[2, :aux_rows, :]
        for n in (1, 3, 0):
            part_copy(n, sibling).wait()

    density_out[0] = (
        parts[0, :aux_rows, :] + parts[1, :aux_rows, :] + parts[2, :aux_rows, :] + parts[3, :aux_rows, :]
    )
    energy_out[0] = jnp.sum(parts[0, aux_rows:, :])

    @pl.when(core == 1)
    def _():
        for n, (at, size) in enumerate(pieces):
            a_first(n, at, size, up * 2 + 1).wait_send()
            a_second(n, at, size, up * 2 + 1).wait_send()

        @pl.loop(0, steps)
        def _(j):
            cand_forward(j).wait_send()

    for n, (at, size) in enumerate(pieces):
        a_direct(n, at, size).wait_send()
        a_across(n, at, size).wait_send()
        a_forward(n, at, size).wait_send()

    @pl.loop(0, steps)
    def _(j):
        cand_copy(j, 0, 0, sibling).wait_send()
        cand_copy(j, 2, 1, sibling).wait_send()
        b_direct(j).wait_send()
        b_across(j).wait_send()
        b_forward(j).wait_send()


def on_device(blocks, occ_energy, vir_energy, occ_count, vir_count, partner_offset):
    frag_total, occ = occ_energy.shape
    vir = vir_energy.shape[1]
    rows = blocks.shape[1]
    half = occ * vir // 2
    steps = occ // 2
    padded = -(-4 * rows // BLOCK) * BLOCK
    aux_rows = vir // 4
    n_pieces = len(pieces_of(rows))
    vmem = pl.BlockSpec(memory_space=pltpu.VMEM)
    smem = pl.BlockSpec(memory_space=pltpu.SMEM)
    dma = pltpu.SemaphoreType.DMA
    return pl.pallas_call(
        functools.partial(kernel, frag_total),
        out_shape=(
            jax.ShapeDtypeStruct((1,), jnp.float32),
            jax.ShapeDtypeStruct((1, aux_rows, vir), jnp.float32),
        ),
        in_specs=[pl.BlockSpec(memory_space=pl.ANY), smem, vmem, smem, smem, smem],
        out_specs=(smem, vmem),
        scratch_shapes=[
            pltpu.VMEM((padded, half), jnp.bfloat16),
            pltpu.VMEM((rows, half), jnp.bfloat16),
            pltpu.VMEM((steps, padded, vir), jnp.bfloat16),
            pltpu.VMEM((steps, rows, vir), jnp.bfloat16),
            pltpu.VMEM((3, steps, rows, 2 * vir), jnp.bfloat16),
            pltpu.VMEM((vir, padded), jnp.bfloat16),
            pltpu.VMEM((vir, vir), jnp.float32),
            pltpu.VMEM((vir, vir), jnp.float32),
            pltpu.VMEM((4, 2 * aux_rows + 8, vir), jnp.float32),
            pltpu.VMEM((4, 2 * aux_rows + 8, vir), jnp.float32),
            pltpu.VMEM((4, aux_rows + 8, vir), jnp.float32),
            pltpu.VMEM((4, aux_rows + 8, vir), jnp.float32),
            pltpu.VMEM((8, 128), jnp.int32),
            pltpu.VMEM((8, 128), jnp.int32),
            pltpu.SMEM((8, 128), jnp.int32),
            dma((2, n_pieces)),
            dma((2, n_pieces)),
            dma((3, n_pieces)),
            dma((3, n_pieces)),
            dma((2, steps)),
            dma((3, steps)),
            dma((steps,)),
            dma((3, steps)),
            dma((3, steps)),
            dma((3,)),
            dma((3,)),
            dma((3,)),
            dma((4,)),
            dma((4,)),
        ],
        compiler_params=pltpu.CompilerParams(
            collective_id=0, has_side_effects=True, vmem_limit_bytes=60 * 1024 * 1024
        ),
        cost_estimate=pl.CostEstimate(
            flops=2 * 4 * rows * half * half, bytes_accessed=2 * rows * 2 * half, transcendentals=0
        ),
        name="pair_terms",
    )(blocks, occ_energy, vir_energy, occ_count, vir_count, partner_offset)


def solution(mesh):
    placed = (P("frag", "aux", None), P(), P(), P(), P(), P("frag"))
    return jax.shard_map(
        on_device,
        mesh=mesh,
        in_specs=placed,
        out_specs=(P("frag"), P("frag", "aux", None)),
        check_vma=False,
    )
```

```python
import functools

import jax
import jax.numpy as jnp
from jax import lax
from jax.experimental import pallas as pl
from jax.experimental.pallas import tpu as pltpu
from jax.sharding import PartitionSpec as P

LEAD = 2
BLOCK = 256
ROW_FRAGS = 8
MESH = pl.DeviceIdType.MESH


def to_device(src, dst, send_sem, recv_sem, frag, aux):
    return pltpu.make_async_remote_copy(
        src_ref=src,
        dst_ref=dst,
        send_sem=send_sem,
        recv_sem=recv_sem,
        device_id={"frag": frag, "aux": aux},
        device_id_type=MESH,
    )


def place_in_ring(aux, row):
    turn = lax.rem(row, 2)
    at = lax.rem(aux + 4 - turn, 4)
    mate = lax.rem(at + 1 - 2 * lax.rem(at, 2) + turn, 4)
    outer = lax.rem(3 - at + turn, 4)
    return at // 2, lax.rem(at, 2), mate, outer


def kernel(
    frag_total,
    blocks,
    occ_energy_in,
    vir_energy_in,
    occ_count_in,
    vir_count_in,
    offset_in,
    energy_out,
    density_out,
    a_stage,
    transit,
    relay,
    occ_energy,
    vir_energy,
    occ_count,
    vir_count,
    offset,
    a_half,
    b_half,
    b_other,
    b_mine,
    cand,
    a_turned,
    b_turned,
    base,
    keep,
    total,
    landed,
    summed,
    parts,
    off_vectors,
    off_scalars,
    in_sems,
    z_send,
    z_recv,
    a_send,
    a_recv,
    cand_send,
    cand_recv,
    cand_pass,
    b_send,
    b_recv,
    b_share,
    relay_recv,
    off_sems,
    sum_send,
    sum_recv,
    part_send,
    part_recv,
):
    rows = blocks.shape[1]
    steps, padded, vir = a_half.shape
    aux_rows = vir // 4
    chips = frag_total // 2
    grid_rows = frag_total // ROW_FRAGS

    frag = lax.axis_index("frag")
    aux = lax.axis_index("aux")
    core = lax.rem(frag, 2)
    chip = frag // 2
    row = frag // ROW_FRAGS
    up = lax.rem(chip + 1, chips)
    down = lax.rem(chip + chips - 1, chips)
    sibling = chip * 2 + 1 - core
    next_row = lax.rem(frag + ROW_FRAGS, frag_total)
    last_row = lax.rem(frag + frag_total - ROW_FRAGS, frag_total)

    pair, q_half, mate, outer = place_in_ring(aux, row)
    far = lax.rem(aux + 2, 4)
    member = core == pair
    stranger = core != pair
    relay_pair, _, relay_to, _ = place_in_ring(aux, lax.rem(row + grid_rows - 1, grid_rows))
    relays = core == relay_pair
    up_outer = place_in_ring(aux, up * 2 // ROW_FRAGS)[3]
    down_outer = place_in_ring(aux, down * 2 // ROW_FRAGS)[3]

    ins = [
        pltpu.make_async_copy(there, here, in_sems.at[n])
        for n, (there, here) in enumerate(
            (
                (offset_in, offset),
                (occ_energy_in, occ_energy),
                (vir_energy_in, vir_energy),
                (occ_count_in, occ_count),
                (vir_count_in, vir_count),
            )
        )
    ]
    for copy in ins:
        copy.start()

    barrier = pltpu.get_barrier_semaphore()
    greeted = [(sibling, aux)]
    greeted += [(chip * 2 + n, other) for other in (mate, outer) for n in range(2)]
    greeted += [(up * 2 + n, other) for other in (aux, outer, up_outer) for n in range(2)]
    greeted += [(down * 2 + n, other) for other in (aux, outer, down_outer) for n in range(2)]
    greeted += [(next_row, aux), (next_row, mate), (last_row, aux), (last_row, relay_to)]
    for there, other in greeted:
        pl.semaphore_signal(barrier, inc=1, device_id={"frag": there, "aux": other}, device_id_type=MESH)
    pl.semaphore_wait(barrier, len(greeted))

    def rows_of(who):
        return pl.ds(pl.multiple_of(who * rows, 16), rows)

    def two_cols(s):
        return pl.ds(pl.multiple_of(s * 2 * vir, 128), 2 * vir)

    def z_copy(s):
        return to_device(
            blocks.at[0, :, two_cols(s)], a_stage.at[s], z_send.at[s], z_recv.at[s], up * 2 + 1, aux
        )

    def cand_copy(s, slot, n, there):
        src = blocks.at[0, :, two_cols(s)]
        if there is None:
            return pltpu.make_async_copy(src, cand.at[slot, s], cand_recv.at[slot, s])
        return to_device(src, cand.at[slot, s], cand_send.at[n, s], cand_recv.at[slot, s], there, aux)

    def cand_forward(s):
        return to_device(cand.at[2, s], cand.at[1, s], cand_pass.at[s], cand_recv.at[1, s], sibling, aux)

    def a_source(s, core_is, part):
        if core_is == 0:
            return blocks.at[0, :, pl.ds(pl.multiple_of(s * 2 * vir + part * vir, 128), vir)]
        return a_stage.at[s, :, pl.ds(part * vir, vir)]

    def a_own(s, core_is):
        return pltpu.make_async_copy(
            a_source(s, core_is, core_is), a_half.at[s, rows_of(aux)], a_recv.at[0, s]
        )

    def a_copy(s, core_is, part, kind):
        there, other = {0: (sibling, aux), 1: (chip * 2 + part, mate), 2: (chip * 2 + part, outer)}[kind]
        n = 0 if kind == 0 else 1 + part
        return to_device(
            a_source(s, core_is, part),
            a_half.at[s, rows_of(aux)],
            a_send.at[n, s],
            a_recv.at[kind, s],
            there,
            other,
        )

    def a_forward(s):
        here = a_half.at[s, rows_of(outer)]
        return to_device(here, here, a_send.at[3, s], a_recv.at[3, s], frag, mate)

    def a_landing(s, kind, who):
        here = a_half.at[s, rows_of(who)]
        return to_device(here, here, a_send.at[3, s], a_recv.at[kind, s], frag, mate)

    def begin_a(s):
        for core_is in range(2):
            @pl.when(core == core_is)
            def _():
                if core_is == 1:
                    z_copy(s).wait_recv()

                @pl.when(member)
                def _():
                    a_copy(s, core_is, 0, 1).start()
                    a_copy(s, core_is, 1, 1).start()
                    a_copy(s, core_is, 1 - core_is, 0).start()
                    a_own(s, core_is).start()

                @pl.when(stranger)
                def _():
                    a_copy(s, core_is, 0, 2).start()
                    a_copy(s, core_is, 1, 2).start()

    def b_round(s):
        return to_device(b_other.at[s], relay.at[s], b_send.at[0, s], relay_recv.at[s], next_row, aux)

    def b_relay(s):
        return to_device(
            relay.at[s], b_half.at[s, rows_of(aux)], b_send.at[2, s], b_recv.at[1, s], last_row, relay_to
        )

    def b_outer(s):
        return to_device(
            b_other.at[s], b_half.at[s, rows_of(aux)], b_send.at[0, s], b_recv.at[2, s], frag, outer
        )

    def b_through(s):
        return to_device(b_mine.at[s], transit.at[s], b_send.at[1, s], b_recv.at[0, s], frag, outer)

    def b_forward(s):
        return to_device(
            transit.at[s], b_half.at[s, rows_of(outer)], b_send.at[1, s], b_recv.at[3, s], frag, mate
        )

    def b_landing(s, kind, who):
        here = b_half.at[s, rows_of(who)]
        return to_device(here, here, b_share.at[kind, s], b_recv.at[kind, s], sibling, aux)

    def chosen(s, which):
        cols = pl.ds(pl.multiple_of(which * vir, 128), vir)
        one, two, three = (cand[n, s, :, cols] for n in range(3))
        return jnp.where(chosen_at == 1, one, jnp.where(chosen_at == 2, two, three))

    def begin_b(s):
        @pl.when(core == 1)
        def _():
            cand_copy(s, 2, 1, down * 2).wait_recv()
            cand_forward(s).start()
            cand_copy(s, 0, 0, sibling).wait_recv()
            cand_copy(s, 1, 0, None).wait()

        @pl.when(core == 0)
        def _():
            cand_copy(s, 0, 0, sibling).wait_recv()
            cand_copy(s, 2, 1, down * 2 + 1).wait_recv()
            cand_forward(s).wait_recv()

        b_other[s] = chosen(s, 1 - q_half)

        @pl.when(member)
        def _():
            b_round(s).start()
            b_half[s, rows_of(aux), :] = chosen(s, q_half)
            b_landing(s, 0, aux).start()

        @pl.when(stranger)
        def _():
            b_outer(s).start()
            b_mine[s] = chosen(s, q_half)
            b_through(s).start()

    def pass_on(s):
        a_landing(s, 2, outer).wait_recv()
        a_forward(s).start()

        @pl.when(member)
        def _():
            b_through(s).wait_recv()
            b_forward(s).start()

        @pl.when(relays)
        def _():
            b_round(s).wait_recv()
            b_relay(s).start()

    def gather(s):
        @pl.when(member)
        def _():
            for kind, who in ((2, outer), (1, mate), (3, far)):
                b_landing(s, kind, who).wait_recv()
                b_landing(s, kind, who).start()
            for core_is in range(2):
                @pl.when(core == core_is)
                def _():
                    a_own(s, core_is).wait()

        @pl.when(stranger)
        def _():
            a_landing(s, 0, aux).wait_recv()
            for kind, who in ((0, aux), (2, outer), (1, mate), (3, far)):
                b_landing(s, kind, who).wait_recv()

        a_landing(s, 1, mate).wait_recv()
        a_landing(s, 3, far).wait_recv()

    ins[0].wait()

    @pl.when(core == 1)
    def _():
        @pl.loop(0, steps)
        def _(s):
            z_copy(s).start()

    @pl.loop(0, steps)
    def _(s):
        @pl.when(core == 0)
        def _():
            cand_copy(s, 2, 1, down * 2 + 1).start()
            cand_copy(s, 0, 0, sibling).start()

        @pl.when(core == 1)
        def _():
            cand_copy(s, 2, 1, down * 2).start()
            cand_copy(s, 0, 0, sibling).start()
            cand_copy(s, 1, 0, None).start()

    def off_copy(n):
        if n == 0:
            return to_device(
                off_vectors.at[0], off_vectors.at[1], off_sems.at[0], off_sems.at[1], up * 2 + 1, aux
            )
        return to_device(off_vectors.at[1], off_vectors.at[2], off_sems.at[2], off_sems.at[3], sibling, aux)

    def off_read(n):
        return pltpu.make_async_copy(off_vectors.at[n], off_scalars.at[n - 1], off_sems.at[3 + n])

    own_offset = jnp.full(off_vectors.shape[1:], offset[0], jnp.int32)

    @pl.when(core == 0)
    def _():
        off_vectors[1] = own_offset

    @pl.when(core == 1)
    def _():
        off_vectors[0] = own_offset
        off_copy(0).start()

    begin_a(0)

    @pl.when(core == 1)
    def _():
        off_copy(0).wait()

    @pl.when(member)
    def _():
        off_copy(1).start()
        off_vectors[2] = off_vectors[1]

    off_read(1).start()
    off_read(1).wait()
    chosen_at = off_scalars[0, 0, 0]
    begin_b(0)

    @pl.when(member)
    def _():
        off_copy(1).wait_send()

    @pl.when(stranger)
    def _():
        off_copy(1).wait_recv()

    off_read(2).start()
    for n in range(1, LEAD):
        begin_a(n)
        begin_b(n)

    if padded > 4 * rows:
        for half in (a_half, b_half):
            @pl.loop(0, steps)
            def _(s):
                half[s, 4 * rows :, :] = jnp.zeros((padded - 4 * rows, vir), jnp.bfloat16)

    off_read(2).wait()
    distance = off_scalars[1, 0, 0]
    for copy in ins[1:]:
        copy.wait()
    leader = jnp.where(pair == 0, chip * 2, lax.rem(chip * 2 + frag_total - 1, frag_total))
    partner = jnp.minimum(leader + distance, frag_total - 1)
    valid = leader + distance < frag_total
    leader_occ = occ_count[leader]
    partner_occ = occ_count[partner]
    leader_vir = vir_count[leader]
    partner_vir = vir_count[partner]

    leader_levels = vir_energy[pl.ds(leader, 1), :]
    partner_levels = vir_energy[pl.ds(partner, 1), :]
    row_ids = lax.broadcasted_iota(jnp.int32, (vir, vir), 0)
    col_ids = lax.broadcasted_iota(jnp.int32, (vir, vir), 1)
    base[0] = -leader_levels - jnp.broadcast_to(partner_levels, (vir, vir)).T
    base[1] = -partner_levels - jnp.broadcast_to(leader_levels, (vir, vir)).T
    keep[0] = jnp.where((row_ids < partner_vir) & (col_ids < leader_vir), 1.0, 0.0)
    keep[1] = jnp.where((row_ids < leader_vir) & (col_ids < partner_vir), 1.0, 0.0)
    total[...] = jnp.zeros(total.shape, jnp.float32)
    pass_on(0)

    def tile(i, j, way):
        lead_occ = 2 * i + core
        part_occ = 2 * j + q_half
        ok = jnp.logical_and(valid, jnp.logical_and(lead_occ < leader_occ, part_occ < partner_occ))
        level = occ_energy[lead_occ, leader] + occ_energy[part_occ, partner]
        turned, straight = (b_turned, a_half.at[i]) if way == 0 else (a_turned, b_half.at[j])
        integrals = jnp.dot(turned[...], straight[...], preferred_element_type=jnp.float32)
        amplitude = integrals * (keep[way] * jnp.where(ok, 1.0, 0.0)) / (base[way] + level)
        energy = amplitude * integrals
        rounded = amplitude.astype(jnp.bfloat16)
        of_cols = lax.dot_general(
            rounded, rounded, (((0,), (0,)), ((), ())), preferred_element_type=jnp.float32
        )
        of_rows = lax.dot_general(
            rounded, rounded, (((1,), (1,)), ((), ())), preferred_element_type=jnp.float32
        )
        first, second = (of_cols, of_rows) if way == 0 else (of_rows, of_cols)
        for n in range(4):
            piece = slice(n * aux_rows, (n + 1) * aux_rows)
            total[n, :aux_rows, :] += first[piece]
            total[n, aux_rows : 2 * aux_rows, :] += second[piece]
        total[0, 2 * aux_rows :, :] += energy.reshape(vir // 8, 8, vir).sum(0)

    def work(s):
        for at in range(0, padded, BLOCK):
            b_turned[:, at : at + BLOCK] = b_half[s, at : at + BLOCK, :].T
            a_turned[:, at : at + BLOCK] = a_half[s, at : at + BLOCK, :].T

        @pl.loop(0, s + 1)
        def _(i):
            tile(i, s, 0)

        @pl.loop(0, s)
        def _(j):
            tile(s, j, 1)

    @pl.loop(0, steps)
    def _(s):
        @pl.when(s + LEAD < steps)
        def _():
            begin_a(s + LEAD)
            begin_b(s + LEAD)

        @pl.when(s + 1 < steps)
        def _():
            pass_on(s + 1)

        gather(s)
        work(s)

    for n in range(1, 4):
        total[n, 2 * aux_rows :, :] = total[0, 2 * aux_rows :, :]
    column = jnp.where(member, aux, outer)
    who = q_half * 2 + core

    def sum_copy(n, going):
        there, other, quarter, sender = (
            (sibling, aux, jnp.where(member, outer, aux), q_half * 2 + 1 - core),
            (chip * 2 + pair, mate, mate, (1 - q_half) * 2 + pair),
            (chip * 2 + 1 - pair, mate, far, (1 - q_half) * 2 + 1 - pair),
        )[n]
        slot = who if going else sender
        return to_device(total.at[quarter], landed.at[slot], sum_send.at[n], sum_recv.at[slot], there, other)

    for n in (1, 2, 0):
        sum_copy(n, True).start()
    landed[who] = total[column]
    for n in (0, 1, 2):
        sum_copy(n, True).wait_send()
        sum_copy(n, False).wait_recv()
    sums = landed[0] + landed[1] + landed[2] + landed[3]
    summed[0, :aux_rows, :] = sums[:aux_rows]
    summed[0, aux_rows:, :] = sums[2 * aux_rows :]
    for n in range(1, 4):
        summed[n, :aux_rows, :] = jnp.where(distance == n, sums[aux_rows : 2 * aux_rows], 0.0)

    def part_copy(n):
        there = (
            jnp.where(pair == 0, chip * 2, down * 2 + 1),
            jnp.where(pair == 0, chip * 2 + 1, chip * 2),
            jnp.where(pair == 0, up * 2, chip * 2 + 1),
            jnp.where(pair == 0, up * 2 + 1, up * 2),
        )[n]
        if n == 0:
            src, dst = summed.at[0], parts.at[0]
        else:
            src, dst = summed.at[n, pl.ds(0, aux_rows)], parts.at[n, pl.ds(0, aux_rows)]
        return to_device(src, dst, part_send.at[n], part_recv.at[n], there, column)

    for n in (0, 2):
        stays = jnp.logical_and(member, core == n // 2)

        @pl.when(jnp.logical_not(stays))
        def _():
            part_copy(n).start()

        @pl.when(stays)
        def _():
            parts[n] = summed[n]

    for n in (1, 3):
        part_copy(n).start()
    for n in (1, 3):
        part_copy(n).wait()
    for n in (0, 2):
        stays = jnp.logical_and(member, core == n // 2)

        @pl.when(jnp.logical_not(stays))
        def _():
            part_copy(n).wait()

    density_out[0] = (
        parts[0, :aux_rows, :] + parts[1, :aux_rows, :] + parts[2, :aux_rows, :] + parts[3, :aux_rows, :]
    )
    energy_out[0] = jnp.sum(parts[0, aux_rows:, :])

    @pl.loop(0, steps)
    def _(s):
        cand_copy(s, 0, 0, sibling).wait_send()
        cand_copy(s, 2, 1, sibling).wait_send()
        a_forward(s).wait_send()
        for core_is in range(2):
            @pl.when(core == core_is)
            def _():
                a_copy(s, core_is, 0, 1).wait_send()
                a_copy(s, core_is, 1, 1).wait_send()

                @pl.when(member)
                def _():
                    a_copy(s, core_is, 1 - core_is, 0).wait_send()

        @pl.when(core == 1)
        def _():
            z_copy(s).wait_send()
            cand_forward(s).wait_send()

        @pl.when(member)
        def _():
            for kind, who_is in enumerate((aux, mate, outer, far)):
                b_landing(s, kind, who_is).wait_send()

        b_round(s).wait_send()
        b_through(s).wait_send()

        @pl.when(relays)
        def _():
            b_relay(s).wait_send()


def on_device(blocks, occ_energy, vir_energy, occ_count, vir_count, partner_offset):
    frag_total, occ = occ_energy.shape
    vir = vir_energy.shape[1]
    rows = blocks.shape[1]
    steps = occ // 2
    padded = -(-4 * rows // BLOCK) * BLOCK
    aux_rows = vir // 4
    vmem = pl.BlockSpec(memory_space=pltpu.VMEM)
    smem = pl.BlockSpec(memory_space=pltpu.SMEM)
    anywhere = pl.BlockSpec(memory_space=pl.ANY)
    dma = pltpu.SemaphoreType.DMA
    results = pl.pallas_call(
        functools.partial(kernel, frag_total),
        out_shape=(
            jax.ShapeDtypeStruct((1,), jnp.float32),
            jax.ShapeDtypeStruct((1, aux_rows, vir), jnp.float32),
            jax.ShapeDtypeStruct((steps, rows, 2 * vir), jnp.bfloat16),
            jax.ShapeDtypeStruct((steps, rows, vir), jnp.bfloat16),
            jax.ShapeDtypeStruct((steps, rows, vir), jnp.bfloat16),
        ),
        in_specs=[anywhere] * 6,
        out_specs=(smem, vmem, anywhere, anywhere, anywhere),
        scratch_shapes=[
            pltpu.SMEM((occ, frag_total), jnp.float32),
            pltpu.VMEM((frag_total, vir), jnp.float32),
            pltpu.SMEM((frag_total,), jnp.int32),
            pltpu.SMEM((frag_total,), jnp.int32),
            pltpu.SMEM((1,), jnp.int32),
            pltpu.VMEM((steps, padded, vir), jnp.bfloat16),
            pltpu.VMEM((steps, padded, vir), jnp.bfloat16),
            pltpu.VMEM((steps, rows, vir), jnp.bfloat16),
            pltpu.VMEM((steps, rows, vir), jnp.bfloat16),
            pltpu.VMEM((3, steps, rows, 2 * vir), jnp.bfloat16),
            pltpu.VMEM((vir, padded), jnp.bfloat16),
            pltpu.VMEM((vir, padded), jnp.bfloat16),
            pltpu.VMEM((2, vir, vir), jnp.float32),
            pltpu.VMEM((2, vir, vir), jnp.float32),
            pltpu.VMEM((4, 2 * aux_rows + 8, vir), jnp.float32),
            pltpu.VMEM((4, 2 * aux_rows + 8, vir), jnp.float32),
            pltpu.VMEM((4, aux_rows + 8, vir), jnp.float32),
            pltpu.VMEM((4, aux_rows + 8, vir), jnp.float32),
            pltpu.VMEM((3, 8, 128), jnp.int32),
            pltpu.SMEM((2, 8, 128), jnp.int32),
            dma((5,)),
            dma((steps,)),
            dma((steps,)),
            dma((4, steps)),
            dma((4, steps)),
            dma((2, steps)),
            dma((3, steps)),
            dma((steps,)),
            dma((3, steps)),
            dma((4, steps)),
            dma((4, steps)),
            dma((steps,)),
            dma((6,)),
            dma((3,)),
            dma((4,)),
            dma((4,)),
            dma((4,)),
        ],
        compiler_params=pltpu.CompilerParams(
            collective_id=0, has_side_effects=True, vmem_limit_bytes=60 * 1024 * 1024
        ),
        cost_estimate=pl.CostEstimate(
            flops=2 * 4 * rows * (occ * vir // 2) ** 2, bytes_accessed=2 * rows * occ * vir, transcendentals=0
        ),
        name="pair_terms",
    )(blocks, occ_energy.T, vir_energy, occ_count, vir_count, partner_offset)
    return results[0], results[1]


def solution(mesh):
    placed = (P("frag", "aux", None), P(), P(), P(), P(), P("frag"))
    return jax.shard_map(
        on_device,
        mesh=mesh,
        in_specs=placed,
        out_specs=(P("frag"), P("frag", "aux", None)),
        check_vma=False,
    )
```

```python
import functools

import jax
import jax.numpy as jnp
from jax import lax
from jax.experimental import pallas as pl
from jax.experimental.pallas import tpu as pltpu
from jax.sharding import PartitionSpec as P

START = (
    ("z_up", 0),
    ("z_down", 0),
    ("a", 0),
    ("z_up", 1),
    ("a", 1),
    ("z_up", 2),
    ("b", 0),
    ("z_down", 1),
    ("pass_a", 0),
    ("a", 2),
    ("z_up", 3),
    ("z_down", 2),
    ("b", 1),
    ("pass_a", 1),
    ("pass_b", 0),
    ("gather_a", 0),
)
ORDER = (
    ("z_up", 4),
    ("a", 3),
    ("z_down", 3),
    ("b", 2),
    ("pass_b", 1),
    ("pass_a", 2),
    ("gather_a", 1),
    ("gather_b", 0),
    ("work", 0),
)
BLOCK = 256
ROW_FRAGS = 8
MESH = pl.DeviceIdType.MESH


def to_device(src, dst, send_sem, recv_sem, frag, aux):
    return pltpu.make_async_remote_copy(
        src_ref=src,
        dst_ref=dst,
        send_sem=send_sem,
        recv_sem=recv_sem,
        device_id={"frag": frag, "aux": aux},
        device_id_type=MESH,
    )


def place_in_ring(aux, row):
    turn = lax.rem(row, 2)
    at = lax.rem(aux + 4 - turn, 4)
    mate = lax.rem(at + 1 - 2 * lax.rem(at, 2) + turn, 4)
    outer = lax.rem(3 - at + turn, 4)
    return at // 2, lax.rem(at, 2), mate, outer


def kernel(
    frag_total,
    blocks,
    occ_energy_in,
    vir_energy_in,
    occ_count_in,
    vir_count_in,
    offset_in,
    energy_out,
    density_out,
    a_stage,
    transit,
    relay,
    occ_energy,
    vir_energy,
    occ_count,
    vir_count,
    offset,
    a_half,
    b_half,
    b_other,
    b_mine,
    cand,
    a_turned,
    b_turned,
    base,
    keep,
    total,
    landed,
    summed,
    parts,
    off_vectors,
    off_scalars,
    in_sems,
    z_send,
    z_recv,
    a_send,
    a_recv,
    cand_send,
    cand_recv,
    cand_pass,
    b_send,
    b_recv,
    b_share,
    relay_recv,
    off_sems,
    sum_send,
    sum_recv,
    part_send,
    part_recv,
):
    rows = blocks.shape[1]
    steps, padded, vir = a_half.shape
    aux_rows = vir // 4
    chips = frag_total // 2
    grid_rows = frag_total // ROW_FRAGS

    frag = lax.axis_index("frag")
    aux = lax.axis_index("aux")
    core = lax.rem(frag, 2)
    chip = frag // 2
    row = frag // ROW_FRAGS
    up = lax.rem(chip + 1, chips)
    down = lax.rem(chip + chips - 1, chips)
    sibling = chip * 2 + 1 - core
    next_row = lax.rem(frag + ROW_FRAGS, frag_total)
    last_row = lax.rem(frag + frag_total - ROW_FRAGS, frag_total)

    pair, q_half, mate, outer = place_in_ring(aux, row)
    far = lax.rem(aux + 2, 4)
    member = core == pair
    stranger = core != pair
    relay_pair, _, relay_to, _ = place_in_ring(aux, lax.rem(row + grid_rows - 1, grid_rows))
    relays = core == relay_pair
    up_outer = place_in_ring(aux, up * 2 // ROW_FRAGS)[3]
    down_outer = place_in_ring(aux, down * 2 // ROW_FRAGS)[3]

    ins = [
        pltpu.make_async_copy(there, here, in_sems.at[n])
        for n, (there, here) in enumerate(
            (
                (offset_in, offset),
                (occ_energy_in, occ_energy),
                (vir_energy_in, vir_energy),
                (occ_count_in, occ_count),
                (vir_count_in, vir_count),
            )
        )
    ]
    for copy in ins:
        copy.start()

    barrier = pltpu.get_barrier_semaphore()
    greeted = [(sibling, aux)]
    greeted += [(chip * 2 + n, other) for other in (mate, outer) for n in range(2)]
    greeted += [(up * 2 + n, other) for other in (aux, outer, up_outer) for n in range(2)]
    greeted += [(down * 2 + n, other) for other in (aux, outer, down_outer) for n in range(2)]
    greeted += [(next_row, aux), (next_row, mate), (last_row, aux), (last_row, relay_to)]
    for there, other in greeted:
        pl.semaphore_signal(barrier, inc=1, device_id={"frag": there, "aux": other}, device_id_type=MESH)
    pl.semaphore_wait(barrier, len(greeted))

    def rows_of(who):
        return pl.ds(pl.multiple_of(who * rows, 16), rows)

    def two_cols(s):
        return pl.ds(pl.multiple_of(s * 2 * vir, 128), 2 * vir)

    def z_copy(s):
        return to_device(
            blocks.at[0, :, two_cols(s)], a_stage.at[s], z_send.at[s], z_recv.at[s], up * 2 + 1, aux
        )

    def cand_copy(s, slot, n, there):
        src = blocks.at[0, :, two_cols(s)]
        if there is None:
            return pltpu.make_async_copy(src, cand.at[slot, s], cand_recv.at[slot, s])
        return to_device(src, cand.at[slot, s], cand_send.at[n, s], cand_recv.at[slot, s], there, aux)

    def cand_forward(s):
        return to_device(cand.at[2, s], cand.at[1, s], cand_pass.at[s], cand_recv.at[1, s], sibling, aux)

    def z_up(s):
        @pl.when(core == 1)
        def _():
            z_copy(s).start()

    def z_down(s):
        @pl.when(core == 0)
        def _():
            cand_copy(s, 2, 1, down * 2 + 1).start()
            cand_copy(s, 0, 0, sibling).start()

        @pl.when(core == 1)
        def _():
            cand_copy(s, 2, 1, down * 2).start()
            cand_copy(s, 0, 0, sibling).start()
            cand_copy(s, 1, 0, None).start()

    def a_source(s, core_is, part):
        if core_is == 0:
            return blocks.at[0, :, pl.ds(pl.multiple_of(s * 2 * vir + part * vir, 128), vir)]
        return a_stage.at[s, :, pl.ds(part * vir, vir)]

    def a_own(s, core_is):
        return pltpu.make_async_copy(
            a_source(s, core_is, core_is), a_half.at[s, rows_of(aux)], a_recv.at[0, s]
        )

    def a_copy(s, core_is, part, kind):
        there, other = {0: (sibling, aux), 1: (chip * 2 + part, mate), 2: (chip * 2 + part, outer)}[kind]
        n = 0 if kind == 0 else 1 + part
        return to_device(
            a_source(s, core_is, part),
            a_half.at[s, rows_of(aux)],
            a_send.at[n, s],
            a_recv.at[kind, s],
            there,
            other,
        )

    def a_forward(s):
        here = a_half.at[s, rows_of(outer)]
        return to_device(here, here, a_send.at[3, s], a_recv.at[3, s], frag, mate)

    def a_landing(s, kind, who):
        here = a_half.at[s, rows_of(who)]
        return to_device(here, here, a_send.at[3, s], a_recv.at[kind, s], frag, mate)

    def begin_a(s):
        for core_is in range(2):
            @pl.when(core == core_is)
            def _():
                if core_is == 1:
                    z_copy(s).wait_recv()

                @pl.when(member)
                def _():
                    a_copy(s, core_is, 0, 1).start()
                    a_copy(s, core_is, 1, 1).start()
                    a_copy(s, core_is, 1 - core_is, 0).start()
                    a_own(s, core_is).start()

                @pl.when(stranger)
                def _():
                    a_copy(s, core_is, 0, 2).start()
                    a_copy(s, core_is, 1, 2).start()

    def b_round(s):
        return to_device(b_other.at[s], relay.at[s], b_send.at[0, s], relay_recv.at[s], next_row, aux)

    def b_relay(s):
        return to_device(
            relay.at[s], b_half.at[s, rows_of(aux)], b_send.at[2, s], b_recv.at[1, s], last_row, relay_to
        )

    def b_outer(s):
        return to_device(
            b_other.at[s], b_half.at[s, rows_of(aux)], b_send.at[0, s], b_recv.at[2, s], frag, outer
        )

    def b_through(s):
        return to_device(b_mine.at[s], transit.at[s], b_send.at[1, s], b_recv.at[0, s], frag, outer)

    def b_forward(s):
        return to_device(
            transit.at[s], b_half.at[s, rows_of(outer)], b_send.at[1, s], b_recv.at[3, s], frag, mate
        )

    def b_landing(s, kind, who):
        here = b_half.at[s, rows_of(who)]
        return to_device(here, here, b_share.at[kind, s], b_recv.at[kind, s], sibling, aux)

    def chosen(s, which):
        cols = pl.ds(pl.multiple_of(which * vir, 128), vir)
        one, two, three = (cand[n, s, :, cols] for n in range(3))
        chosen_at = off_scalars[0, 0, 0]
        return jnp.where(chosen_at == 1, one, jnp.where(chosen_at == 2, two, three))

    def begin_b(s):
        @pl.when(core == 1)
        def _():
            cand_copy(s, 2, 1, down * 2).wait_recv()
            cand_forward(s).start()
            cand_copy(s, 0, 0, sibling).wait_recv()
            cand_copy(s, 1, 0, None).wait()

        @pl.when(core == 0)
        def _():
            cand_copy(s, 0, 0, sibling).wait_recv()
            cand_copy(s, 2, 1, down * 2 + 1).wait_recv()
            cand_forward(s).wait_recv()

        b_other[s] = chosen(s, 1 - q_half)

        @pl.when(member)
        def _():
            b_round(s).start()
            b_half[s, rows_of(aux), :] = chosen(s, q_half)
            b_landing(s, 0, aux).start()

        @pl.when(stranger)
        def _():
            b_outer(s).start()
            b_mine[s] = chosen(s, q_half)
            b_through(s).start()

    def pass_a(s):
        a_landing(s, 2, outer).wait_recv()
        a_forward(s).start()

    def pass_b(s):
        @pl.when(member)
        def _():
            b_through(s).wait_recv()
            b_forward(s).start()

        @pl.when(relays)
        def _():
            b_round(s).wait_recv()
            b_relay(s).start()

    def gather_a(s):
        @pl.when(member)
        def _():
            for core_is in range(2):
                @pl.when(core == core_is)
                def _():
                    a_own(s, core_is).wait()

        @pl.when(stranger)
        def _():
            a_landing(s, 0, aux).wait_recv()

        a_landing(s, 1, mate).wait_recv()
        a_landing(s, 3, far).wait_recv()

    def gather_b(s):
        @pl.when(member)
        def _():
            for kind, who in ((2, outer), (1, mate), (3, far)):
                b_landing(s, kind, who).wait_recv()
                b_landing(s, kind, who).start()

        @pl.when(stranger)
        def _():
            for kind, who in ((0, aux), (2, outer), (1, mate), (3, far)):
                b_landing(s, kind, who).wait_recv()

    ins[0].wait()

    def off_copy(n):
        if n == 0:
            return to_device(
                off_vectors.at[0], off_vectors.at[1], off_sems.at[0], off_sems.at[1], up * 2 + 1, aux
            )
        return to_device(off_vectors.at[1], off_vectors.at[2], off_sems.at[2], off_sems.at[3], sibling, aux)

    def off_read(n):
        return pltpu.make_async_copy(off_vectors.at[n], off_scalars.at[n - 1], off_sems.at[3 + n])

    own_offset = jnp.full(off_vectors.shape[1:], offset[0], jnp.int32)

    @pl.when(core == 0)
    def _():
        off_vectors[1] = own_offset

    @pl.when(core == 1)
    def _():
        off_vectors[0] = own_offset
        off_copy(0).start()

    def know_offsets():
        @pl.when(core == 1)
        def _():
            off_copy(0).wait()

        @pl.when(member)
        def _():
            off_copy(1).start()
            off_vectors[2] = off_vectors[1]

        off_read(1).start()
        off_read(1).wait()

    stages = {
        "z_up": z_up,
        "z_down": z_down,
        "a": begin_a,
        "b": begin_b,
        "pass_a": pass_a,
        "pass_b": pass_b,
        "gather_a": gather_a,
        "gather_b": gather_b,
    }
    for name, n in START:
        if (name, n) == ("b", 0):
            know_offsets()
        stages[name](n)

    @pl.when(member)
    def _():
        off_copy(1).wait_send()

    @pl.when(stranger)
    def _():
        off_copy(1).wait_recv()

    off_read(2).start()
    if padded > 4 * rows:
        for half in (a_half, b_half):
            @pl.loop(0, steps)
            def _(s):
                half[s, 4 * rows :, :] = jnp.zeros((padded - 4 * rows, vir), jnp.bfloat16)

    off_read(2).wait()
    distance = off_scalars[1, 0, 0]
    for copy in ins[1:]:
        copy.wait()
    leader = jnp.where(pair == 0, chip * 2, lax.rem(chip * 2 + frag_total - 1, frag_total))
    partner = jnp.minimum(leader + distance, frag_total - 1)
    valid = leader + distance < frag_total
    leader_occ = occ_count[leader]
    partner_occ = occ_count[partner]
    leader_vir = vir_count[leader]
    partner_vir = vir_count[partner]

    leader_levels = vir_energy[pl.ds(leader, 1), :]
    partner_levels = vir_energy[pl.ds(partner, 1), :]
    row_ids = lax.broadcasted_iota(jnp.int32, (vir, vir), 0)
    col_ids = lax.broadcasted_iota(jnp.int32, (vir, vir), 1)
    base[0] = -leader_levels - jnp.broadcast_to(partner_levels, (vir, vir)).T
    base[1] = -partner_levels - jnp.broadcast_to(leader_levels, (vir, vir)).T
    keep[0] = jnp.where((row_ids < partner_vir) & (col_ids < leader_vir), 1.0, 0.0)
    keep[1] = jnp.where((row_ids < leader_vir) & (col_ids < partner_vir), 1.0, 0.0)
    total[...] = jnp.zeros(total.shape, jnp.float32)

    def tile(i, j, way):
        lead_occ = 2 * i + core
        part_occ = 2 * j + q_half
        ok = jnp.logical_and(valid, jnp.logical_and(lead_occ < leader_occ, part_occ < partner_occ))
        level = occ_energy[lead_occ, leader] + occ_energy[part_occ, partner]
        turned, straight = (b_turned, a_half.at[i]) if way == 0 else (a_turned, b_half.at[j])
        integrals = jnp.dot(turned[...], straight[...], preferred_element_type=jnp.float32)
        amplitude = integrals * (keep[way] * jnp.where(ok, 1.0, 0.0)) / (base[way] + level)
        energy = amplitude * integrals
        rounded = amplitude.astype(jnp.bfloat16)
        of_cols = lax.dot_general(
            rounded, rounded, (((0,), (0,)), ((), ())), preferred_element_type=jnp.float32
        )
        of_rows = lax.dot_general(
            rounded, rounded, (((1,), (1,)), ((), ())), preferred_element_type=jnp.float32
        )
        first, second = (of_cols, of_rows) if way == 0 else (of_rows, of_cols)
        for n in range(4):
            piece = slice(n * aux_rows, (n + 1) * aux_rows)
            total[n, :aux_rows, :] += first[piece]
            total[n, aux_rows : 2 * aux_rows, :] += second[piece]
        total[0, 2 * aux_rows :, :] += energy.reshape(vir // 8, 8, vir).sum(0)

    def work(s):
        ahead = s + 1 < steps
        for at in range(0, padded, BLOCK):
            b_turned[:, at : at + BLOCK] = b_half[s, at : at + BLOCK, :].T
        columns = jnp.minimum(s + 2, steps)

        @pl.loop(0, columns // 2)
        def _(n):
            tile(2 * n, s, 0)
            tile(2 * n + 1, s, 0)

        @pl.when(lax.rem(columns, 2) == 1)
        def _():
            tile(columns - 1, s, 0)

        @pl.when(ahead)
        def _():
            for at in range(0, padded, BLOCK):
                a_turned[:, at : at + BLOCK] = a_half[s + 1, at : at + BLOCK, :].T

            @pl.loop(0, s // 2)
            def _(n):
                tile(s + 1, 2 * n, 1)
                tile(s + 1, 2 * n + 1, 1)

            @pl.when(lax.rem(s, 2) == 1)
            def _():
                tile(s + 1, s - 1, 1)

    stages["work"] = work

    @pl.loop(0, steps)
    def _(s):
        for name, lead in ORDER:
            @pl.when(s + lead < steps)
            def _():
                stages[name](s + lead)

    for n in range(1, 4):
        total[n, 2 * aux_rows :, :] = total[0, 2 * aux_rows :, :]
    column = jnp.where(member, aux, outer)
    who = q_half * 2 + core

    def sum_copy(n, going):
        there, other, quarter, sender = (
            (sibling, aux, jnp.where(member, outer, aux), q_half * 2 + 1 - core),
            (chip * 2 + pair, mate, mate, (1 - q_half) * 2 + pair),
            (chip * 2 + 1 - pair, mate, far, (1 - q_half) * 2 + 1 - pair),
        )[n]
        slot = who if going else sender
        return to_device(total.at[quarter], landed.at[slot], sum_send.at[n], sum_recv.at[slot], there, other)

    for n in (1, 2, 0):
        sum_copy(n, True).start()
    landed[who] = total[column]
    for n in (0, 1, 2):
        sum_copy(n, True).wait_send()
        sum_copy(n, False).wait_recv()
    sums = landed[0] + landed[1] + landed[2] + landed[3]
    summed[0, :aux_rows, :] = sums[:aux_rows]
    summed[0, aux_rows:, :] = sums[2 * aux_rows :]
    for n in range(1, 4):
        summed[n, :aux_rows, :] = jnp.where(distance == n, sums[aux_rows : 2 * aux_rows], 0.0)

    def part_copy(n):
        there = (
            jnp.where(pair == 0, chip * 2, down * 2 + 1),
            jnp.where(pair == 0, chip * 2 + 1, chip * 2),
            jnp.where(pair == 0, up * 2, chip * 2 + 1),
            jnp.where(pair == 0, up * 2 + 1, up * 2),
        )[n]
        if n == 0:
            src, dst = summed.at[0], parts.at[0]
        else:
            src, dst = summed.at[n, pl.ds(0, aux_rows)], parts.at[n, pl.ds(0, aux_rows)]
        return to_device(src, dst, part_send.at[n], part_recv.at[n], there, column)

    for n in (0, 2):
        stays = jnp.logical_and(member, core == n // 2)

        @pl.when(jnp.logical_not(stays))
        def _():
            part_copy(n).start()

        @pl.when(stays)
        def _():
            parts[n] = summed[n]

    for n in (1, 3):
        part_copy(n).start()
    for n in (1, 3):
        part_copy(n).wait()
    for n in (0, 2):
        stays = jnp.logical_and(member, core == n // 2)

        @pl.when(jnp.logical_not(stays))
        def _():
            part_copy(n).wait()

    density_out[0] = (
        parts[0, :aux_rows, :] + parts[1, :aux_rows, :] + parts[2, :aux_rows, :] + parts[3, :aux_rows, :]
    )
    energy_out[0] = jnp.sum(parts[0, aux_rows:, :])

    @pl.loop(0, steps)
    def _(s):
        cand_copy(s, 0, 0, sibling).wait_send()
        cand_copy(s, 2, 1, sibling).wait_send()
        a_forward(s).wait_send()
        for core_is in range(2):
            @pl.when(core == core_is)
            def _():
                a_copy(s, core_is, 0, 1).wait_send()
                a_copy(s, core_is, 1, 1).wait_send()

                @pl.when(member)
                def _():
                    a_copy(s, core_is, 1 - core_is, 0).wait_send()

        @pl.when(core == 1)
        def _():
            z_copy(s).wait_send()
            cand_forward(s).wait_send()

        @pl.when(member)
        def _():
            for kind, who_is in enumerate((aux, mate, outer, far)):
                b_landing(s, kind, who_is).wait_send()

        b_round(s).wait_send()
        b_through(s).wait_send()

        @pl.when(relays)
        def _():
            b_relay(s).wait_send()


def on_device(blocks, occ_energy, vir_energy, occ_count, vir_count, partner_offset):
    frag_total, occ = occ_energy.shape
    vir = vir_energy.shape[1]
    rows = blocks.shape[1]
    steps = occ // 2
    padded = -(-4 * rows // BLOCK) * BLOCK
    aux_rows = vir // 4
    vmem = pl.BlockSpec(memory_space=pltpu.VMEM)
    smem = pl.BlockSpec(memory_space=pltpu.SMEM)
    anywhere = pl.BlockSpec(memory_space=pl.ANY)
    dma = pltpu.SemaphoreType.DMA
    results = pl.pallas_call(
        functools.partial(kernel, frag_total),
        out_shape=(
            jax.ShapeDtypeStruct((1,), jnp.float32),
            jax.ShapeDtypeStruct((1, aux_rows, vir), jnp.float32),
            jax.ShapeDtypeStruct((steps, rows, 2 * vir), jnp.bfloat16),
            jax.ShapeDtypeStruct((steps, rows, vir), jnp.bfloat16),
            jax.ShapeDtypeStruct((steps, rows, vir), jnp.bfloat16),
        ),
        in_specs=[anywhere] * 6,
        out_specs=(smem, vmem, anywhere, anywhere, anywhere),
        scratch_shapes=[
            pltpu.SMEM((occ, frag_total), jnp.float32),
            pltpu.VMEM((frag_total, vir), jnp.float32),
            pltpu.SMEM((frag_total,), jnp.int32),
            pltpu.SMEM((frag_total,), jnp.int32),
            pltpu.SMEM((1,), jnp.int32),
            pltpu.VMEM((steps, padded, vir), jnp.bfloat16),
            pltpu.VMEM((steps, padded, vir), jnp.bfloat16),
            pltpu.VMEM((steps, rows, vir), jnp.bfloat16),
            pltpu.VMEM((steps, rows, vir), jnp.bfloat16),
            pltpu.VMEM((3, steps, rows, 2 * vir), jnp.bfloat16),
            pltpu.VMEM((vir, padded), jnp.bfloat16),
            pltpu.VMEM((vir, padded), jnp.bfloat16),
            pltpu.VMEM((2, vir, vir), jnp.float32),
            pltpu.VMEM((2, vir, vir), jnp.float32),
            pltpu.VMEM((4, 2 * aux_rows + 8, vir), jnp.float32),
            pltpu.VMEM((4, 2 * aux_rows + 8, vir), jnp.float32),
            pltpu.VMEM((4, aux_rows + 8, vir), jnp.float32),
            pltpu.VMEM((4, aux_rows + 8, vir), jnp.float32),
            pltpu.VMEM((3, 8, 128), jnp.int32),
            pltpu.SMEM((2, 8, 128), jnp.int32),
            dma((5,)),
            dma((steps,)),
            dma((steps,)),
            dma((4, steps)),
            dma((4, steps)),
            dma((2, steps)),
            dma((3, steps)),
            dma((steps,)),
            dma((3, steps)),
            dma((4, steps)),
            dma((4, steps)),
            dma((steps,)),
            dma((6,)),
            dma((3,)),
            dma((4,)),
            dma((4,)),
            dma((4,)),
        ],
        compiler_params=pltpu.CompilerParams(
            collective_id=0, has_side_effects=True, vmem_limit_bytes=60 * 1024 * 1024
        ),
        cost_estimate=pl.CostEstimate(
            flops=2 * 4 * rows * (occ * vir // 2) ** 2, bytes_accessed=2 * rows * occ * vir, transcendentals=0
        ),
        name="pair_terms",
    )(blocks, occ_energy.T, vir_energy, occ_count, vir_count, partner_offset)
    return results[0], results[1]


def solution(mesh):
    placed = (P("frag", "aux", None), P(), P(), P(), P(), P("frag"))
    return jax.shard_map(
        on_device,
        mesh=mesh,
        in_specs=placed,
        out_specs=(P("frag"), P("frag", "aux", None)),
        check_vma=False,
    )
```

```python
import functools

import jax
import jax.numpy as jnp
from jax import lax
from jax.experimental import pallas as pl
from jax.experimental.pallas import tpu as pltpu
from jax.sharding import PartitionSpec as P

START = (
    ("z_up", 0),
    ("z_down", 0),
    ("z_down", 1),
    ("a", 0),
    ("z_up", 1),
    ("a", 1),
    ("z_up", 2),
    ("pass_a", 0),
    ("b", 0),
    ("z_down", 2),
    ("a", 2),
    ("z_up", 3),
    ("pass_a", 1),
    ("b", 1),
    ("z_down", 3),
    ("pass_b", 0),
    ("gather_a", 0),
)
ORDER = (
    ("z_up", 4),
    ("a", 3),
    ("b", 2),
    ("z_down", 4),
    ("pass_b", 1),
    ("pass_a", 2),
    ("gather_a", 1),
    ("gather_b", 0),
    ("columns", 0),
    ("across", 0),
)
BLOCK = 256
ROW_FRAGS = 8
MESH = pl.DeviceIdType.MESH


def to_device(src, dst, send_sem, recv_sem, frag, aux):
    return pltpu.make_async_remote_copy(
        src_ref=src,
        dst_ref=dst,
        send_sem=send_sem,
        recv_sem=recv_sem,
        device_id={"frag": frag, "aux": aux},
        device_id_type=MESH,
    )


def place_in_ring(aux, row):
    turn = lax.rem(row, 2)
    at = lax.rem(aux + 4 - turn, 4)
    mate = lax.rem(at + 1 - 2 * lax.rem(at, 2) + turn, 4)
    outer = lax.rem(3 - at + turn, 4)
    return at // 2, lax.rem(at, 2), mate, outer


def kernel(
    frag_total,
    blocks,
    occ_energy_in,
    vir_energy_in,
    occ_count_in,
    vir_count_in,
    offset_in,
    energy_out,
    density_out,
    a_stage,
    transit,
    relay,
    occ_energy,
    vir_energy,
    occ_count,
    vir_count,
    offset,
    a_half,
    b_half,
    b_other,
    b_mine,
    cand,
    a_turned,
    b_turned,
    base,
    keep,
    halves,
    total,
    landed,
    summed,
    parts,
    off_vectors,
    off_scalars,
    in_sems,
    z_send,
    z_recv,
    a_send,
    a_recv,
    cand_send,
    cand_recv,
    cand_pass,
    b_send,
    b_recv,
    b_share,
    relay_recv,
    off_sems,
    sum_send,
    sum_recv,
    part_send,
    part_recv,
):
    rows = blocks.shape[1]
    steps, padded, vir = a_half.shape
    aux_rows = vir // 4
    chips = frag_total // 2
    grid_rows = frag_total // ROW_FRAGS

    frag = lax.axis_index("frag")
    aux = lax.axis_index("aux")
    core = lax.rem(frag, 2)
    chip = frag // 2
    row = frag // ROW_FRAGS
    up = lax.rem(chip + 1, chips)
    down = lax.rem(chip + chips - 1, chips)
    sibling = chip * 2 + 1 - core
    next_row = lax.rem(frag + ROW_FRAGS, frag_total)
    last_row = lax.rem(frag + frag_total - ROW_FRAGS, frag_total)

    pair, q_half, mate, outer = place_in_ring(aux, row)
    far = lax.rem(aux + 2, 4)
    member = core == pair
    stranger = core != pair
    relay_pair, _, relay_to, _ = place_in_ring(aux, lax.rem(row + grid_rows - 1, grid_rows))
    relays = core == relay_pair

    ins = [
        pltpu.make_async_copy(there, here, in_sems.at[n])
        for n, (there, here) in enumerate(
            (
                (offset_in, offset),
                (occ_energy_in, occ_energy),
                (vir_energy_in, vir_energy),
                (occ_count_in, occ_count),
                (vir_count_in, vir_count),
            )
        )
    ]
    for copy in ins:
        copy.start()

    barrier = pltpu.get_barrier_semaphore()
    greeted = [(sibling, aux)]
    greeted += [(chip * 2 + n, other) for other in (mate, outer, far) for n in range(2)]
    greeted += [(there * 2 + n, aux) for there in (up, down) for n in range(2)]
    greeted += [(next_row, aux), (next_row, mate), (last_row, aux), (last_row, relay_to)]
    for there, other in greeted:
        pl.semaphore_signal(barrier, inc=1, device_id={"frag": there, "aux": other}, device_id_type=MESH)
    pl.semaphore_wait(barrier, len(greeted))

    def rows_of(who):
        return pl.ds(pl.multiple_of(who * rows, 16), rows)

    def two_cols(s):
        return pl.ds(pl.multiple_of(s * 2 * vir, 128), 2 * vir)

    def z_copy(s):
        return to_device(
            blocks.at[0, :, two_cols(s)], a_stage.at[s], z_send.at[s], z_recv.at[s], up * 2 + 1, aux
        )

    def cand_copy(s, slot, n, there):
        src = blocks.at[0, :, two_cols(s)]
        if there is None:
            return pltpu.make_async_copy(src, cand.at[slot, s], cand_recv.at[slot, s])
        return to_device(src, cand.at[slot, s], cand_send.at[n, s], cand_recv.at[slot, s], there, aux)

    def cand_forward(s):
        return to_device(cand.at[2, s], cand.at[1, s], cand_pass.at[s], cand_recv.at[1, s], sibling, aux)

    def z_up(s):
        @pl.when(core == 1)
        def _():
            z_copy(s).start()

    def z_down(s):
        @pl.when(core == 0)
        def _():
            cand_copy(s, 2, 1, down * 2 + 1).start()
            cand_copy(s, 0, 0, sibling).start()

        @pl.when(core == 1)
        def _():
            cand_copy(s, 2, 1, down * 2).start()
            cand_copy(s, 0, 0, sibling).start()
            cand_copy(s, 1, 0, None).start()

    def a_source(s, core_is, part):
        if core_is == 0:
            return blocks.at[0, :, pl.ds(pl.multiple_of(s * 2 * vir + part * vir, 128), vir)]
        return a_stage.at[s, :, pl.ds(part * vir, vir)]

    def a_own(s, core_is):
        return pltpu.make_async_copy(
            a_source(s, core_is, core_is), a_half.at[s, rows_of(aux)], a_recv.at[0, s]
        )

    def a_copy(s, core_is, part, kind):
        there, other = {0: (sibling, aux), 1: (chip * 2 + part, mate), 2: (chip * 2 + part, outer)}[kind]
        n = 0 if kind == 0 else 1 + part
        return to_device(
            a_source(s, core_is, part),
            a_half.at[s, rows_of(aux)],
            a_send.at[n, s],
            a_recv.at[kind, s],
            there,
            other,
        )

    def a_forward(s):
        here = a_half.at[s, rows_of(outer)]
        return to_device(here, here, a_send.at[3, s], a_recv.at[3, s], frag, mate)

    def a_landing(s, kind, who):
        here = a_half.at[s, rows_of(who)]
        return to_device(here, here, a_send.at[3, s], a_recv.at[kind, s], frag, mate)

    def begin_a(s):
        for core_is in range(2):
            @pl.when(core == core_is)
            def _():
                if core_is == 1:
                    z_copy(s).wait_recv()

                @pl.when(member)
                def _():
                    a_copy(s, core_is, 0, 1).start()
                    a_copy(s, core_is, 1, 1).start()
                    a_copy(s, core_is, 1 - core_is, 0).start()
                    a_own(s, core_is).start()

                @pl.when(stranger)
                def _():
                    a_copy(s, core_is, 0, 2).start()
                    a_copy(s, core_is, 1, 2).start()

    def b_round(s):
        return to_device(b_other.at[s], relay.at[s], b_send.at[0, s], relay_recv.at[s], next_row, aux)

    def b_relay(s):
        return to_device(
            relay.at[s], b_half.at[s, rows_of(aux)], b_send.at[2, s], b_recv.at[1, s], last_row, relay_to
        )

    def b_outer(s):
        return to_device(
            b_other.at[s], b_half.at[s, rows_of(aux)], b_send.at[0, s], b_recv.at[2, s], frag, outer
        )

    def b_through(s):
        return to_device(b_mine.at[s], transit.at[s], b_send.at[1, s], b_recv.at[0, s], frag, outer)

    def b_forward(s):
        return to_device(
            transit.at[s], b_half.at[s, rows_of(outer)], b_send.at[1, s], b_recv.at[3, s], frag, mate
        )

    def b_landing(s, kind, who):
        here = b_half.at[s, rows_of(who)]
        return to_device(here, here, b_share.at[kind, s], b_recv.at[kind, s], sibling, aux)

    def chosen(s, which):
        cols = pl.ds(pl.multiple_of(which * vir, 128), vir)
        one, two, three = (cand[n, s, :, cols] for n in range(3))
        chosen_at = off_scalars[0, 0, 0]
        return jnp.where(chosen_at == 1, one, jnp.where(chosen_at == 2, two, three))

    def begin_b(s):
        @pl.when(core == 1)
        def _():
            cand_copy(s, 2, 1, down * 2).wait_recv()
            cand_forward(s).start()
            cand_copy(s, 0, 0, sibling).wait_recv()
            cand_copy(s, 1, 0, None).wait()

        @pl.when(core == 0)
        def _():
            cand_copy(s, 0, 0, sibling).wait_recv()
            cand_copy(s, 2, 1, down * 2 + 1).wait_recv()
            cand_forward(s).wait_recv()

        b_other[s] = chosen(s, 1 - q_half)

        @pl.when(member)
        def _():
            b_round(s).start()
            b_half[s, rows_of(aux), :] = chosen(s, q_half)
            b_landing(s, 0, aux).start()

        @pl.when(stranger)
        def _():
            b_outer(s).start()
            b_mine[s] = chosen(s, q_half)
            b_through(s).start()

    def pass_a(s):
        a_landing(s, 2, outer).wait_recv()
        a_forward(s).start()

    def pass_b(s):
        @pl.when(member)
        def _():
            b_through(s).wait_recv()
            b_forward(s).start()

        @pl.when(relays)
        def _():
            b_round(s).wait_recv()
            b_relay(s).start()

    def gather_a(s):
        @pl.when(member)
        def _():
            for core_is in range(2):
                @pl.when(core == core_is)
                def _():
                    a_own(s, core_is).wait()

        @pl.when(stranger)
        def _():
            a_landing(s, 0, aux).wait_recv()

        a_landing(s, 1, mate).wait_recv()
        a_landing(s, 3, far).wait_recv()

    def gather_b(s):
        @pl.when(member)
        def _():
            for kind, who in ((2, outer), (1, mate), (3, far)):
                b_landing(s, kind, who).wait_recv()
                b_landing(s, kind, who).start()

        @pl.when(stranger)
        def _():
            for kind, who in ((0, aux), (2, outer), (1, mate), (3, far)):
                b_landing(s, kind, who).wait_recv()

    ins[0].wait()

    def off_copy(n):
        if n == 0:
            return to_device(
                off_vectors.at[0], off_vectors.at[1], off_sems.at[0], off_sems.at[1], up * 2 + 1, aux
            )
        return to_device(off_vectors.at[1], off_vectors.at[2], off_sems.at[2], off_sems.at[3], sibling, aux)

    def off_read(n):
        return pltpu.make_async_copy(off_vectors.at[n], off_scalars.at[n - 1], off_sems.at[3 + n])

    own_offset = jnp.full(off_vectors.shape[1:], offset[0], jnp.int32)

    @pl.when(core == 0)
    def _():
        off_vectors[1] = own_offset

    @pl.when(core == 1)
    def _():
        off_vectors[0] = own_offset
        off_copy(0).start()

    def know_offsets():
        @pl.when(core == 1)
        def _():
            off_copy(0).wait()

        @pl.when(member)
        def _():
            off_copy(1).start()
            off_vectors[2] = off_vectors[1]

        off_read(1).start()
        off_read(1).wait()

    stages = {
        "z_up": z_up,
        "z_down": z_down,
        "a": begin_a,
        "b": begin_b,
        "pass_a": pass_a,
        "pass_b": pass_b,
        "gather_a": gather_a,
        "gather_b": gather_b,
    }
    for name, n in START:
        if (name, n) == ("b", 0):
            know_offsets()
        stages[name](n)

    @pl.when(member)
    def _():
        off_copy(1).wait_send()

    @pl.when(stranger)
    def _():
        off_copy(1).wait_recv()

    off_read(2).start()
    if padded > 4 * rows:
        for half in (a_half, b_half):
            @pl.loop(0, steps)
            def _(s):
                half[s, 4 * rows :, :] = jnp.zeros((padded - 4 * rows, vir), jnp.bfloat16)

    off_read(2).wait()
    distance = off_scalars[1, 0, 0]
    for copy in ins[1:]:
        copy.wait()
    leader = jnp.where(pair == 0, chip * 2, lax.rem(chip * 2 + frag_total - 1, frag_total))
    partner = jnp.minimum(leader + distance, frag_total - 1)
    valid = leader + distance < frag_total
    leader_occ = occ_count[leader]
    partner_occ = occ_count[partner]
    leader_vir = vir_count[leader]
    partner_vir = vir_count[partner]

    leader_levels = vir_energy[pl.ds(leader, 1), :]
    partner_levels = vir_energy[pl.ds(partner, 1), :]
    row_ids = lax.broadcasted_iota(jnp.int32, (vir, vir), 0)
    col_ids = lax.broadcasted_iota(jnp.int32, (vir, vir), 1)
    base[0] = -leader_levels - jnp.broadcast_to(partner_levels, (vir, vir)).T
    base[1] = -partner_levels - jnp.broadcast_to(leader_levels, (vir, vir)).T
    keep[0] = jnp.where((row_ids < partner_vir) & (col_ids < leader_vir), 1.0, 0.0)
    keep[1] = jnp.where((row_ids < leader_vir) & (col_ids < partner_vir), 1.0, 0.0)
    total[...] = jnp.zeros(total.shape, jnp.float32)

    def amplitudes(i, j, way):
        lead_occ = 2 * i + core
        part_occ = 2 * j + q_half
        ok = jnp.logical_and(valid, jnp.logical_and(lead_occ < leader_occ, part_occ < partner_occ))
        level = occ_energy[lead_occ, leader] + occ_energy[part_occ, partner]
        turned, straight = (b_turned, a_half.at[i]) if way == 0 else (a_turned, b_half.at[j])
        integrals = jnp.dot(turned[...], straight[...], preferred_element_type=jnp.float32)
        amplitude = integrals * (keep[way] * jnp.where(ok, 1.0, 0.0)) / (base[way] + level)
        energy = amplitude * integrals
        total[0, 2 * aux_rows :, :] += energy.reshape(vir // 8, 8, vir).sum(0)
        return amplitude.astype(jnp.bfloat16)

    def squares(rounded, way):
        of_cols, of_rows = 0.0, 0.0
        for each in rounded:
            of_cols += lax.dot_general(each, each, (((0,), (0,)), ((), ())), preferred_element_type=jnp.float32)
            of_rows += lax.dot_general(each, each, (((1,), (1,)), ((), ())), preferred_element_type=jnp.float32)
        first, second = (of_cols, of_rows) if way == 0 else (of_rows, of_cols)
        for n in range(4):
            piece = slice(n * aux_rows, (n + 1) * aux_rows)
            total[n, :aux_rows, :] += first[piece]
            total[n, aux_rows : 2 * aux_rows, :] += second[piece]

    def tiles(count, way, place):
        def two(n):
            for m in range(2):
                halves[m] = amplitudes(*place(2 * n + m), way)

        @pl.when(count > 1)
        def _():
            two(0)

            @pl.loop(1, count // 2)
            def _(n):
                squares([halves[m] for m in range(2)], way)
                two(n)

            squares([halves[m] for m in range(2)], way)

        @pl.when(lax.rem(count, 2) == 1)
        def _():
            squares([amplitudes(*place(count - 1), way)], way)

    def columns(s):
        for at in range(0, padded, BLOCK):
            b_turned[:, at : at + BLOCK] = b_half[s, at : at + BLOCK, :].T
        tiles(jnp.minimum(s + 2, steps), 0, lambda n: (n, s))

    def across(s):
        @pl.when(s + 1 < steps)
        def _():
            for at in range(0, padded, BLOCK):
                a_turned[:, at : at + BLOCK] = a_half[s + 1, at : at + BLOCK, :].T
            tiles(s, 1, lambda n: (s + 1, n))

    stages["columns"] = columns
    stages["across"] = across

    @pl.loop(0, steps)
    def _(s):
        for name, lead in ORDER:
            @pl.when(s + lead < steps)
            def _():
                stages[name](s + lead)

    for n in range(1, 4):
        total[n, 2 * aux_rows :, :] = total[0, 2 * aux_rows :, :]
    who = q_half * 2 + core

    def sum_copy(n):
        column = lax.rem(aux + n, 4)
        there = sibling if n == 0 else chip * 2 + pair
        return to_device(total.at[column], landed.at[who], sum_send.at[n], sum_recv.at[who], there, column)

    def sum_landing(n):
        return to_device(landed.at[n], landed.at[n], sum_send.at[0], sum_recv.at[n], sibling, aux)

    for n in (2, 1, 3):
        sum_copy(n).start()

    @pl.when(stranger)
    def _():
        sum_copy(0).start()

    @pl.when(member)
    def _():
        landed[who] = total[aux]

    @pl.loop(0, steps)
    def _(s):
        cand_copy(s, 0, 0, sibling).wait_send()
        cand_copy(s, 2, 1, sibling).wait_send()
        a_forward(s).wait_send()
        for core_is in range(2):
            @pl.when(core == core_is)
            def _():
                a_copy(s, core_is, 0, 1).wait_send()
                a_copy(s, core_is, 1, 1).wait_send()

                @pl.when(member)
                def _():
                    a_copy(s, core_is, 1 - core_is, 0).wait_send()

        @pl.when(core == 1)
        def _():
            z_copy(s).wait_send()
            cand_forward(s).wait_send()

        @pl.when(member)
        def _():
            for kind, who_is in enumerate((aux, mate, outer, far)):
                b_landing(s, kind, who_is).wait_send()

        b_round(s).wait_send()
        b_through(s).wait_send()

        @pl.when(relays)
        def _():
            b_relay(s).wait_send()

    for n in range(1, 4):
        sum_copy(n).wait_send()

    @pl.when(stranger)
    def _():
        sum_copy(0).wait_send()

    for n in range(4):
        @pl.when(jnp.logical_or(stranger, who != n))
        def _():
            sum_landing(n).wait_recv()

    own_distance = off_scalars[0, 0, 0]
    sums = landed[0] + landed[1] + landed[2] + landed[3]
    summed[0, :aux_rows, :] = sums[:aux_rows]
    summed[0, aux_rows:, :] = sums[2 * aux_rows :]
    for n in range(1, 4):
        summed[n, :aux_rows, :] = jnp.where(own_distance == n, sums[aux_rows : 2 * aux_rows], 0.0)

    def part_copy(n):
        there = (
            down * 2 + 1,
            sibling,
            up * 2,
            jnp.where(core == 0, up * 2 + 1, up * 2),
        )[n]
        if n == 0:
            src, dst = summed.at[0], parts.at[0]
        else:
            src, dst = summed.at[n, pl.ds(0, aux_rows)], parts.at[n, pl.ds(0, aux_rows)]
        return to_device(src, dst, part_send.at[n], part_recv.at[n], there, aux)

    for n in (0, 2):
        stays = core == n // 2

        @pl.when(core != n // 2)
        def _():
            part_copy(n).start()

        @pl.when(stays)
        def _():
            parts[n] = summed[n]

    for n in (1, 3):
        part_copy(n).start()
    for n in (1, 3):
        part_copy(n).wait()
    for n in (0, 2):
        stays = core == n // 2

        @pl.when(core != n // 2)
        def _():
            part_copy(n).wait()

    density_out[0] = (
        parts[0, :aux_rows, :] + parts[1, :aux_rows, :] + parts[2, :aux_rows, :] + parts[3, :aux_rows, :]
    )
    energy_out[0] = jnp.sum(parts[0, aux_rows:, :])


def on_device(blocks, occ_energy, vir_energy, occ_count, vir_count, partner_offset):
    frag_total, occ = occ_energy.shape
    vir = vir_energy.shape[1]
    rows = blocks.shape[1]
    steps = occ // 2
    padded = -(-4 * rows // BLOCK) * BLOCK
    aux_rows = vir // 4
    vmem = pl.BlockSpec(memory_space=pltpu.VMEM)
    smem = pl.BlockSpec(memory_space=pltpu.SMEM)
    anywhere = pl.BlockSpec(memory_space=pl.ANY)
    dma = pltpu.SemaphoreType.DMA
    results = pl.pallas_call(
        functools.partial(kernel, frag_total),
        out_shape=(
            jax.ShapeDtypeStruct((1,), jnp.float32),
            jax.ShapeDtypeStruct((1, aux_rows, vir), jnp.float32),
            jax.ShapeDtypeStruct((steps, rows, 2 * vir), jnp.bfloat16),
            jax.ShapeDtypeStruct((steps, rows, vir), jnp.bfloat16),
            jax.ShapeDtypeStruct((steps, rows, vir), jnp.bfloat16),
        ),
        in_specs=[anywhere] * 6,
        out_specs=(smem, vmem, anywhere, anywhere, anywhere),
        scratch_shapes=[
            pltpu.SMEM((occ, frag_total), jnp.float32),
            pltpu.VMEM((frag_total, vir), jnp.float32),
            pltpu.SMEM((frag_total,), jnp.int32),
            pltpu.SMEM((frag_total,), jnp.int32),
            pltpu.SMEM((1,), jnp.int32),
            pltpu.VMEM((steps, padded, vir), jnp.bfloat16),
            pltpu.VMEM((steps, padded, vir), jnp.bfloat16),
            pltpu.VMEM((steps, rows, vir), jnp.bfloat16),
            pltpu.VMEM((steps, rows, vir), jnp.bfloat16),
            pltpu.VMEM((3, steps, rows, 2 * vir), jnp.bfloat16),
            pltpu.VMEM((vir, padded), jnp.bfloat16),
            pltpu.VMEM((vir, padded), jnp.bfloat16),
            pltpu.VMEM((2, vir, vir), jnp.float32),
            pltpu.VMEM((2, vir, vir), jnp.float32),
            pltpu.VMEM((2, vir, vir), jnp.bfloat16),
            pltpu.VMEM((4, 2 * aux_rows + 8, vir), jnp.float32),
            pltpu.VMEM((4, 2 * aux_rows + 8, vir), jnp.float32),
            pltpu.VMEM((4, aux_rows + 8, vir), jnp.float32),
            pltpu.VMEM((4, aux_rows + 8, vir), jnp.float32),
            pltpu.VMEM((3, 8, 128), jnp.int32),
            pltpu.SMEM((2, 8, 128), jnp.int32),
            dma((5,)),
            dma((steps,)),
            dma((steps,)),
            dma((4, steps)),
            dma((4, steps)),
            dma((2, steps)),
            dma((3, steps)),
            dma((steps,)),
            dma((3, steps)),
            dma((4, steps)),
            dma((4, steps)),
            dma((steps,)),
            dma((6,)),
            dma((4,)),
            dma((4,)),
            dma((4,)),
            dma((4,)),
        ],
        compiler_params=pltpu.CompilerParams(
            collective_id=0, has_side_effects=True, vmem_limit_bytes=60 * 1024 * 1024
        ),
        cost_estimate=pl.CostEstimate(
            flops=2 * 4 * rows * (occ * vir // 2) ** 2, bytes_accessed=2 * rows * occ * vir, transcendentals=0
        ),
        name="pair_terms",
    )(blocks, occ_energy.T, vir_energy, occ_count, vir_count, partner_offset)
    return results[0], results[1]


def solution(mesh):
    placed = (P("frag", "aux", None), P(), P(), P(), P(), P("frag"))
    return jax.shard_map(
        on_device,
        mesh=mesh,
        in_specs=placed,
        out_specs=(P("frag"), P("frag", "aux", None)),
        check_vma=False,
    )
```

```python
import collections
import functools

import jax
import jax.numpy as jnp
from jax import lax
from jax.experimental import pallas as pl
from jax.experimental.pallas import tpu as pltpu
from jax.sharding import PartitionSpec as P

START = (
    ("z_down", 0),
    ("z_down", 1),
    ("z_up", 0),
    ("z_down", 2),
    ("z_up", 1),
    ("a", 0),
    ("z_up", 2),
    ("a", 1),
    ("z_up", 3),
    ("pass_a", 0),
    ("b", 0),
    ("z_down", 3),
    ("a", 2),
    ("z_up", 4),
    ("pass_a", 1),
    ("b", 1),
    ("z_down", 4),
    ("a", 3),
    ("z_up", 5),
    ("pass_b", 0),
    ("pass_a", 2),
    ("b", 2),
    ("z_down", 5),
    ("a", 4),
    ("z_up", 6),
    ("pass_a", 3),
    ("b", 3),
    ("z_down", 6),
    ("a", 5),
    ("z_up", 7),
    ("pass_b", 1),
    ("z_down", 7),
    ("gather_a", 0),
    ("gather_a", 1),
    ("gather_a", 2),
)
ORDER = (
    ("z_up", 8),
    ("a", 6),
    ("b", 4),
    ("z_down", 8),
    ("pass_a", 4),
    ("gather_a", 3),
    ("pass_b", 2),
    ("across", 0),
    ("gather_b", 0),
    ("columns", 0),
)
BLOCK = 256
ROW_FRAGS = 8
MESH = pl.DeviceIdType.MESH


Part = collections.namedtuple("Part", "step half")


def to_device(src, dst, send_sem, recv_sem, frag, aux):
    return pltpu.make_async_remote_copy(
        src_ref=src,
        dst_ref=dst,
        send_sem=send_sem,
        recv_sem=recv_sem,
        device_id={"frag": frag, "aux": aux},
        device_id_type=MESH,
    )


def place_in_ring(aux, row):
    turn = lax.rem(row, 2)
    at = lax.rem(aux + 4 - turn, 4)
    mate = lax.rem(at + 1 - 2 * lax.rem(at, 2) + turn, 4)
    outer = lax.rem(3 - at + turn, 4)
    return at // 2, lax.rem(at, 2), mate, outer


def kernel(
    frag_total,
    blocks,
    occ_energy_in,
    vir_energy_in,
    occ_count_in,
    vir_count_in,
    offset_in,
    energy_out,
    density_out,
    a_stage,
    transit,
    relay,
    occ_energy,
    vir_energy,
    occ_count,
    vir_count,
    offset,
    a_half,
    b_half,
    b_other,
    b_mine,
    cand,
    a_turned,
    b_turned,
    base,
    keep,
    halves,
    total,
    landed,
    summed,
    parts,
    off_vectors,
    off_scalars,
    in_sems,
    z_send,
    z_recv,
    a_send,
    a_recv,
    cand_send,
    cand_recv,
    cand_pass,
    b_send,
    b_recv,
    b_share,
    relay_recv,
    off_sems,
    sum_send,
    sum_recv,
    part_send,
    part_recv,
):
    rows = blocks.shape[1]
    steps, padded, vir = a_half.shape
    aux_rows = vir // 4
    chips = frag_total // 2
    grid_rows = frag_total // ROW_FRAGS

    frag = lax.axis_index("frag")
    aux = lax.axis_index("aux")
    core = lax.rem(frag, 2)
    chip = frag // 2
    row = frag // ROW_FRAGS
    up = lax.rem(chip + 1, chips)
    down = lax.rem(chip + chips - 1, chips)
    sibling = chip * 2 + 1 - core
    next_row = lax.rem(frag + ROW_FRAGS, frag_total)
    last_row = lax.rem(frag + frag_total - ROW_FRAGS, frag_total)

    pair, q_half, mate, outer = place_in_ring(aux, row)
    far = lax.rem(aux + 2, 4)
    member = core == pair
    stranger = core != pair
    relay_pair, _, relay_to, _ = place_in_ring(aux, lax.rem(row + grid_rows - 1, grid_rows))
    relays = core == relay_pair

    ins = [
        pltpu.make_async_copy(there, here, in_sems.at[n])
        for n, (there, here) in enumerate(
            (
                (offset_in, offset),
                (occ_energy_in, occ_energy),
                (vir_energy_in, vir_energy),
                (occ_count_in, occ_count),
                (vir_count_in, vir_count),
            )
        )
    ]
    for copy in ins:
        copy.start()

    barrier = pltpu.get_barrier_semaphore()
    greeted = [(sibling, aux)]
    greeted += [(chip * 2 + n, other) for other in (mate, outer, far) for n in range(2)]
    greeted += [(there * 2 + n, aux) for there in (up, down) for n in range(2)]
    greeted += [(next_row, aux), (next_row, mate), (last_row, aux), (last_row, relay_to)]
    for there, other in greeted:
        pl.semaphore_signal(barrier, inc=1, device_id={"frag": there, "aux": other}, device_id_type=MESH)
    pl.semaphore_wait(barrier, len(greeted))

    first_rows = -(-rows // 32) * 16

    def own(s):
        return pl.ds(0, first_rows) if s.half == 0 else pl.ds(first_rows, rows - first_rows)

    def rows_of(who, s):
        here = own(s)
        return pl.ds(pl.multiple_of(who * rows + here.start, 16), here.size)

    def two_cols(s):
        return pl.ds(pl.multiple_of(s * 2 * vir, 128), 2 * vir)

    def z_copy(s):
        return to_device(
            blocks.at[0, own(s), two_cols(s.step)], a_stage.at[s.step, own(s)], z_send.at[s.step, s.half], z_recv.at[s.step, s.half], up * 2 + 1, aux
        )

    def cand_copy(s, slot, n, there):
        src = blocks.at[0, own(s), two_cols(s.step)]
        if there is None:
            return pltpu.make_async_copy(src, cand.at[slot, s.step, own(s)], cand_recv.at[slot, s.step, s.half])
        return to_device(src, cand.at[slot, s.step, own(s)], cand_send.at[n, s.step, s.half], cand_recv.at[slot, s.step, s.half], there, aux)

    def cand_forward(s):
        return to_device(cand.at[2, s.step, own(s)], cand.at[1, s.step, own(s)], cand_pass.at[s.step, s.half], cand_recv.at[1, s.step, s.half], sibling, aux)

    def z_up(s):
        @pl.when(core == 1)
        def _():
            z_copy(s).start()

    def z_down(s):
        @pl.when(core == 0)
        def _():
            cand_copy(s, 2, 1, down * 2 + 1).start()
            cand_copy(s, 0, 0, sibling).start()

        @pl.when(core == 1)
        def _():
            cand_copy(s, 2, 1, down * 2).start()
            cand_copy(s, 0, 0, sibling).start()
            cand_copy(s, 1, 0, None).start()

    def a_source(s, core_is, part):
        if core_is == 0:
            return blocks.at[0, own(s), pl.ds(pl.multiple_of(s.step * 2 * vir + part * vir, 128), vir)]
        return a_stage.at[s.step, own(s), pl.ds(part * vir, vir)]

    def a_own(s, core_is):
        return pltpu.make_async_copy(
            a_source(s, core_is, core_is), a_half.at[s.step, rows_of(aux, s)], a_recv.at[0, s.step, s.half]
        )

    def a_copy(s, core_is, part, kind):
        there, other = {0: (sibling, aux), 1: (chip * 2 + part, mate), 2: (chip * 2 + part, outer)}[kind]
        n = 0 if kind == 0 else 1 + part
        return to_device(
            a_source(s, core_is, part),
            a_half.at[s.step, rows_of(aux, s)],
            a_send.at[n, s.step, s.half],
            a_recv.at[kind, s.step, s.half],
            there,
            other,
        )

    def a_forward(s):
        here = a_half.at[s.step, rows_of(outer, s)]
        return to_device(here, here, a_send.at[3, s.step, s.half], a_recv.at[3, s.step, s.half], frag, mate)

    def a_landing(s, kind, who):
        here = a_half.at[s.step, rows_of(who, s)]
        return to_device(here, here, a_send.at[3, s.step, s.half], a_recv.at[kind, s.step, s.half], frag, mate)

    def begin_a(s):
        for core_is in range(2):
            @pl.when(core == core_is)
            def _():
                if core_is == 1:
                    z_copy(s).wait_recv()

                @pl.when(member)
                def _():
                    a_copy(s, core_is, 0, 1).start()
                    a_copy(s, core_is, 1, 1).start()
                    a_copy(s, core_is, 1 - core_is, 0).start()
                    a_own(s, core_is).start()

                @pl.when(stranger)
                def _():
                    a_copy(s, core_is, 0, 2).start()
                    a_copy(s, core_is, 1, 2).start()

    def b_round(s):
        return to_device(b_other.at[s.step, own(s)], relay.at[s.step, own(s)], b_send.at[0, s.step, s.half], relay_recv.at[s.step, s.half], next_row, aux)

    def b_relay(s):
        return to_device(
            relay.at[s.step, own(s)], b_half.at[s.step, rows_of(aux, s)], b_send.at[2, s.step, s.half], b_recv.at[1, s.step, s.half], last_row, relay_to
        )

    def b_outer(s):
        return to_device(
            b_other.at[s.step, own(s)], b_half.at[s.step, rows_of(aux, s)], b_send.at[0, s.step, s.half], b_recv.at[2, s.step, s.half], frag, outer
        )

    def b_through(s):
        return to_device(b_mine.at[s.step, own(s)], transit.at[s.step, own(s)], b_send.at[1, s.step, s.half], b_recv.at[0, s.step, s.half], frag, outer)

    def b_forward(s):
        return to_device(
            transit.at[s.step, own(s)], b_half.at[s.step, rows_of(outer, s)], b_send.at[1, s.step, s.half], b_recv.at[3, s.step, s.half], frag, mate
        )

    def b_landing(s, kind, who):
        here = b_half.at[s.step, rows_of(who, s)]
        return to_device(here, here, b_share.at[kind, s.step, s.half], b_recv.at[kind, s.step, s.half], sibling, aux)

    def chosen(s, which):
        cols = pl.ds(pl.multiple_of(which * vir, 128), vir)
        one, two, three = (cand[n, s.step, own(s), cols] for n in range(3))
        chosen_at = off_scalars[0, 0, 0]
        return jnp.where(chosen_at == 1, one, jnp.where(chosen_at == 2, two, three))

    def begin_b(s):
        @pl.when(core == 1)
        def _():
            cand_copy(s, 2, 1, down * 2).wait_recv()
            cand_forward(s).start()
            cand_copy(s, 0, 0, sibling).wait_recv()
            cand_copy(s, 1, 0, None).wait()

        @pl.when(core == 0)
        def _():
            cand_copy(s, 0, 0, sibling).wait_recv()
            cand_copy(s, 2, 1, down * 2 + 1).wait_recv()
            cand_forward(s).wait_recv()

        b_other[s.step, own(s), :] = chosen(s, 1 - q_half)

        @pl.when(member)
        def _():
            b_round(s).start()
            b_half[s.step, rows_of(aux, s), :] = chosen(s, q_half)
            b_landing(s, 0, aux).start()

        @pl.when(stranger)
        def _():
            b_outer(s).start()
            b_mine[s.step, own(s), :] = chosen(s, q_half)
            b_through(s).start()

    def pass_a(s):
        a_landing(s, 2, outer).wait_recv()
        a_forward(s).start()

    def pass_b(s):
        @pl.when(member)
        def _():
            b_through(s).wait_recv()
            b_forward(s).start()

        @pl.when(relays)
        def _():
            b_round(s).wait_recv()
            b_relay(s).start()

    def gather_a(s):
        @pl.when(member)
        def _():
            for core_is in range(2):
                @pl.when(core == core_is)
                def _():
                    a_own(s, core_is).wait()

        @pl.when(stranger)
        def _():
            a_landing(s, 0, aux).wait_recv()

        a_landing(s, 1, mate).wait_recv()
        a_landing(s, 3, far).wait_recv()

    def gather_b(s):
        @pl.when(member)
        def _():
            for kind, who in ((2, outer), (1, mate), (3, far)):
                b_landing(s, kind, who).wait_recv()
                b_landing(s, kind, who).start()

        @pl.when(stranger)
        def _():
            for kind, who in ((0, aux), (2, outer), (1, mate), (3, far)):
                b_landing(s, kind, who).wait_recv()

    ins[0].wait()

    def off_copy(n):
        if n == 0:
            return to_device(
                off_vectors.at[0], off_vectors.at[1], off_sems.at[0], off_sems.at[1], up * 2 + 1, aux
            )
        return to_device(off_vectors.at[1], off_vectors.at[2], off_sems.at[2], off_sems.at[3], sibling, aux)

    def off_read(n):
        return pltpu.make_async_copy(off_vectors.at[n], off_scalars.at[n - 1], off_sems.at[3 + n])

    own_offset = jnp.full(off_vectors.shape[1:], offset[0], jnp.int32)

    @pl.when(core == 0)
    def _():
        off_vectors[1] = own_offset

    @pl.when(core == 1)
    def _():
        off_vectors[0] = own_offset
        off_copy(0).start()

    def know_offsets():
        @pl.when(core == 1)
        def _():
            off_copy(0).wait()

        @pl.when(member)
        def _():
            off_copy(1).start()
            off_vectors[2] = off_vectors[1]

        off_read(1).start()
        off_read(1).wait()

    stages = {
        "z_up": z_up,
        "z_down": z_down,
        "a": begin_a,
        "b": begin_b,
        "pass_a": pass_a,
        "pass_b": pass_b,
        "gather_a": gather_a,
        "gather_b": gather_b,
    }
    for name, n in START:
        if (name, n) == ("b", 0):
            know_offsets()
        stages[name](Part(n // 2, n % 2))

    @pl.when(member)
    def _():
        off_copy(1).wait_send()

    @pl.when(stranger)
    def _():
        off_copy(1).wait_recv()

    off_read(2).start()
    if padded > 4 * rows:
        for half in (a_half, b_half):
            @pl.loop(0, steps)
            def _(s):
                half[s, 4 * rows :, :] = jnp.zeros((padded - 4 * rows, vir), jnp.bfloat16)

    off_read(2).wait()
    distance = off_scalars[1, 0, 0]
    for copy in ins[1:]:
        copy.wait()
    leader = jnp.where(pair == 0, chip * 2, lax.rem(chip * 2 + frag_total - 1, frag_total))
    partner = jnp.minimum(leader + distance, frag_total - 1)
    valid = leader + distance < frag_total
    leader_occ = occ_count[leader]
    partner_occ = occ_count[partner]
    leader_vir = vir_count[leader]
    partner_vir = vir_count[partner]

    leader_levels = vir_energy[pl.ds(leader, 1), :]
    partner_levels = vir_energy[pl.ds(partner, 1), :]
    row_ids = lax.broadcasted_iota(jnp.int32, (vir, vir), 0)
    col_ids = lax.broadcasted_iota(jnp.int32, (vir, vir), 1)
    base[0] = -leader_levels - jnp.broadcast_to(partner_levels, (vir, vir)).T
    base[1] = -partner_levels - jnp.broadcast_to(leader_levels, (vir, vir)).T
    keep[0] = jnp.where((row_ids < partner_vir) & (col_ids < leader_vir), 1.0, 0.0)
    keep[1] = jnp.where((row_ids < leader_vir) & (col_ids < partner_vir), 1.0, 0.0)
    total[...] = jnp.zeros(total.shape, jnp.float32)

    def amplitudes(i, j, way):
        lead_occ = 2 * i + core
        part_occ = 2 * j + q_half
        ok = jnp.logical_and(valid, jnp.logical_and(lead_occ < leader_occ, part_occ < partner_occ))
        level = occ_energy[lead_occ, leader] + occ_energy[part_occ, partner]
        turned, straight = (b_turned, a_half.at[i]) if way == 0 else (a_turned, b_half.at[j])
        integrals = jnp.dot(turned[...], straight[...], preferred_element_type=jnp.float32)
        amplitude = integrals * (keep[way] * jnp.where(ok, 1.0, 0.0)) / (base[way] + level)
        energy = amplitude * integrals
        total[0, 2 * aux_rows :, :] += energy.reshape(vir // 8, 8, vir).sum(0)
        return amplitude.astype(jnp.bfloat16)

    def squares(rounded, way):
        of_cols, of_rows = 0.0, 0.0
        for each in rounded:
            of_cols += lax.dot_general(each, each, (((0,), (0,)), ((), ())), preferred_element_type=jnp.float32)
            of_rows += lax.dot_general(each, each, (((1,), (1,)), ((), ())), preferred_element_type=jnp.float32)
        first, second = (of_cols, of_rows) if way == 0 else (of_rows, of_cols)
        for n in range(4):
            piece = slice(n * aux_rows, (n + 1) * aux_rows)
            total[n, :aux_rows, :] += first[piece]
            total[n, aux_rows : 2 * aux_rows, :] += second[piece]

    def tiles(count, way, place):
        def two(n):
            for m in range(2):
                halves[m] = amplitudes(*place(2 * n + m), way)

        @pl.when(count > 1)
        def _():
            two(0)

            @pl.loop(1, count // 2)
            def _(n):
                squares([halves[m] for m in range(2)], way)
                two(n)

            squares([halves[m] for m in range(2)], way)

        @pl.when(lax.rem(count, 2) == 1)
        def _():
            squares([amplitudes(*place(count - 1), way)], way)

    def columns(s):
        for at in range(0, padded, BLOCK):
            b_turned[:, at : at + BLOCK] = b_half[s, at : at + BLOCK, :].T
        tiles(jnp.minimum(s + 2, steps), 0, lambda n: (n, s))

    def across(s):
        @pl.when(s + 1 < steps)
        def _():
            for at in range(0, padded, BLOCK):
                a_turned[:, at : at + BLOCK] = a_half[s + 1, at : at + BLOCK, :].T
            tiles(s, 1, lambda n: (s + 1, n))

    stages["columns"] = columns
    stages["across"] = across

    @pl.loop(0, steps)
    def _(s):
        for half in range(2):
            for name, lead in ORDER:
                part = Part(s + (half + lead) // 2, (half + lead) % 2)
                if name in ("columns", "across"):
                    if part.half != (name == "columns"):
                        continue
                    part = part.step

                @pl.when(s + (half + lead) // 2 < steps)
                def _():
                    stages[name](part)

    for n in range(1, 4):
        total[n, 2 * aux_rows :, :] = total[0, 2 * aux_rows :, :]
    who = q_half * 2 + core

    def sum_copy(n):
        column = lax.rem(aux + n, 4)
        there = sibling if n == 0 else chip * 2 + pair
        return to_device(total.at[column], landed.at[who], sum_send.at[n], sum_recv.at[who], there, column)

    def sum_landing(n):
        return to_device(landed.at[n], landed.at[n], sum_send.at[0], sum_recv.at[n], sibling, aux)

    for n in (2, 1, 3):
        sum_copy(n).start()

    @pl.when(stranger)
    def _():
        sum_copy(0).start()

    @pl.when(member)
    def _():
        landed[who] = total[aux]

    @pl.loop(0, steps)
    def _(step):
        for s in (Part(step, 0), Part(step, 1)):
            cand_copy(s, 0, 0, sibling).wait_send()
            cand_copy(s, 2, 1, sibling).wait_send()
            a_forward(s).wait_send()
            for core_is in range(2):
                @pl.when(core == core_is)
                def _():
                    a_copy(s, core_is, 0, 1).wait_send()
                    a_copy(s, core_is, 1, 1).wait_send()

                    @pl.when(member)
                    def _():
                        a_copy(s, core_is, 1 - core_is, 0).wait_send()

            @pl.when(core == 1)
            def _():
                z_copy(s).wait_send()
                cand_forward(s).wait_send()

            @pl.when(member)
            def _():
                for kind, who_is in enumerate((aux, mate, outer, far)):
                    b_landing(s, kind, who_is).wait_send()

            b_round(s).wait_send()
            b_through(s).wait_send()

            @pl.when(relays)
            def _():
                b_relay(s).wait_send()

    for n in range(1, 4):
        sum_copy(n).wait_send()

    @pl.when(stranger)
    def _():
        sum_copy(0).wait_send()

    for n in range(4):
        @pl.when(jnp.logical_or(stranger, who != n))
        def _():
            sum_landing(n).wait_recv()

    own_distance = off_scalars[0, 0, 0]
    sums = landed[0] + landed[1] + landed[2] + landed[3]
    summed[0, :aux_rows, :] = sums[:aux_rows]
    summed[0, aux_rows:, :] = sums[2 * aux_rows :]
    for n in range(1, 4):
        summed[n, :aux_rows, :] = jnp.where(own_distance == n, sums[aux_rows : 2 * aux_rows], 0.0)

    def part_copy(n):
        there = (
            down * 2 + 1,
            sibling,
            up * 2,
            jnp.where(core == 0, up * 2 + 1, up * 2),
        )[n]
        if n == 0:
            src, dst = summed.at[0], parts.at[0]
        else:
            src, dst = summed.at[n, pl.ds(0, aux_rows)], parts.at[n, pl.ds(0, aux_rows)]
        return to_device(src, dst, part_send.at[n], part_recv.at[n], there, aux)

    for n in (0, 2):
        stays = core == n // 2

        @pl.when(core != n // 2)
        def _():
            part_copy(n).start()

        @pl.when(stays)
        def _():
            parts[n] = summed[n]

    for n in (1, 3):
        part_copy(n).start()
    for n in (1, 3):
        part_copy(n).wait()
    for n in (0, 2):
        stays = core == n // 2

        @pl.when(core != n // 2)
        def _():
            part_copy(n).wait()

    density_out[0] = (
        parts[0, :aux_rows, :] + parts[1, :aux_rows, :] + parts[2, :aux_rows, :] + parts[3, :aux_rows, :]
    )
    energy_out[0] = jnp.sum(parts[0, aux_rows:, :])


def on_device(blocks, occ_energy, vir_energy, occ_count, vir_count, partner_offset):
    frag_total, occ = occ_energy.shape
    vir = vir_energy.shape[1]
    rows = blocks.shape[1]
    steps = occ // 2
    padded = -(-4 * rows // BLOCK) * BLOCK
    aux_rows = vir // 4
    vmem = pl.BlockSpec(memory_space=pltpu.VMEM)
    smem = pl.BlockSpec(memory_space=pltpu.SMEM)
    anywhere = pl.BlockSpec(memory_space=pl.ANY)
    dma = pltpu.SemaphoreType.DMA
    results = pl.pallas_call(
        functools.partial(kernel, frag_total),
        out_shape=(
            jax.ShapeDtypeStruct((1,), jnp.float32),
            jax.ShapeDtypeStruct((1, aux_rows, vir), jnp.float32),
            jax.ShapeDtypeStruct((steps, rows, 2 * vir), jnp.bfloat16),
            jax.ShapeDtypeStruct((steps, rows, vir), jnp.bfloat16),
            jax.ShapeDtypeStruct((steps, rows, vir), jnp.bfloat16),
        ),
        in_specs=[anywhere] * 6,
        out_specs=(smem, vmem, anywhere, anywhere, anywhere),
        scratch_shapes=[
            pltpu.SMEM((occ, frag_total), jnp.float32),
            pltpu.VMEM((frag_total, vir), jnp.float32),
            pltpu.SMEM((frag_total,), jnp.int32),
            pltpu.SMEM((frag_total,), jnp.int32),
            pltpu.SMEM((1,), jnp.int32),
            pltpu.VMEM((steps, padded, vir), jnp.bfloat16),
            pltpu.VMEM((steps, padded, vir), jnp.bfloat16),
            pltpu.VMEM((steps, rows, vir), jnp.bfloat16),
            pltpu.VMEM((steps, rows, vir), jnp.bfloat16),
            pltpu.VMEM((3, steps, rows, 2 * vir), jnp.bfloat16),
            pltpu.VMEM((vir, padded), jnp.bfloat16),
            pltpu.VMEM((vir, padded), jnp.bfloat16),
            pltpu.VMEM((2, vir, vir), jnp.float32),
            pltpu.VMEM((2, vir, vir), jnp.float32),
            pltpu.VMEM((2, vir, vir), jnp.bfloat16),
            pltpu.VMEM((4, 2 * aux_rows + 8, vir), jnp.float32),
            pltpu.VMEM((4, 2 * aux_rows + 8, vir), jnp.float32),
            pltpu.VMEM((4, aux_rows + 8, vir), jnp.float32),
            pltpu.VMEM((4, aux_rows + 8, vir), jnp.float32),
            pltpu.VMEM((3, 8, 128), jnp.int32),
            pltpu.SMEM((2, 8, 128), jnp.int32),
            dma((5,)),
            dma((steps, 2)),
            dma((steps, 2)),
            dma((4, steps, 2)),
            dma((4, steps, 2)),
            dma((2, steps, 2)),
            dma((3, steps, 2)),
            dma((steps, 2)),
            dma((3, steps, 2)),
            dma((4, steps, 2)),
            dma((4, steps, 2)),
            dma((steps, 2)),
            dma((6,)),
            dma((4,)),
            dma((4,)),
            dma((4,)),
            dma((4,)),
        ],
        compiler_params=pltpu.CompilerParams(
            collective_id=0, has_side_effects=True, vmem_limit_bytes=60 * 1024 * 1024
        ),
        cost_estimate=pl.CostEstimate(
            flops=2 * 4 * rows * (occ * vir // 2) ** 2, bytes_accessed=2 * rows * occ * vir, transcendentals=0
        ),
        name="pair_terms",
    )(blocks, occ_energy.T, vir_energy, occ_count, vir_count, partner_offset)
    return results[0], results[1]


def solution(mesh):
    placed = (P("frag", "aux", None), P(), P(), P(), P(), P("frag"))
    return jax.shard_map(
        on_device,
        mesh=mesh,
        in_specs=placed,
        out_specs=(P("frag"), P("frag", "aux", None)),
        check_vma=False,
    )
```

```python
import collections
import functools

import jax
import jax.numpy as jnp
from jax import lax
from jax.experimental import pallas as pl
from jax.experimental.pallas import tpu as pltpu
from jax.sharding import PartitionSpec as P

START = (
    ("z_down", 0),
    ("z_down", 1),
    ("z_up", 0),
    ("z_down", 2),
    ("z_up", 1),
    ("a", 0),
    ("z_up", 2),
    ("a", 1),
    ("z_up", 3),
    ("pass_a", 0),
    ("b", 0),
    ("z_down", 3),
    ("a", 2),
    ("z_up", 4),
    ("pass_a", 1),
    ("b", 1),
    ("z_down", 4),
    ("a", 3),
    ("z_up", 5),
    ("pass_b", 0),
    ("pass_a", 2),
    ("b", 2),
    ("z_down", 5),
    ("a", 4),
    ("z_up", 6),
    ("pass_a", 3),
    ("b", 3),
    ("z_down", 6),
    ("a", 5),
    ("z_up", 7),
    ("pass_b", 1),
    ("z_down", 7),
    ("gather_a", 0),
    ("gather_a", 1),
    ("gather_a", 2),
)
ORDER = (
    ("z_up", 8),
    ("a", 6),
    ("b", 4),
    ("z_down", 8),
    ("pass_a", 4),
    ("gather_a", 3),
    ("pass_b", 2),
    ("across", 0),
    ("gather_b", 0),
    ("columns", 0),
)
BLOCK = 256
KEPT = 3
ROW_FRAGS = 8
MESH = pl.DeviceIdType.MESH


Part = collections.namedtuple("Part", "step half")


def to_device(src, dst, send_sem, recv_sem, frag, aux):
    return pltpu.make_async_remote_copy(
        src_ref=src,
        dst_ref=dst,
        send_sem=send_sem,
        recv_sem=recv_sem,
        device_id={"frag": frag, "aux": aux},
        device_id_type=MESH,
    )


def place_in_ring(aux, row):
    turn = lax.rem(row, 2)
    at = lax.rem(aux + 4 - turn, 4)
    mate = lax.rem(at + 1 - 2 * lax.rem(at, 2) + turn, 4)
    outer = lax.rem(3 - at + turn, 4)
    return at // 2, lax.rem(at, 2), mate, outer


def kernel(
    frag_total,
    blocks,
    occ_energy_in,
    vir_energy_in,
    occ_count_in,
    vir_count_in,
    offset_in,
    energy_out,
    density_out,
    a_stage,
    transit,
    relay,
    occ_energy,
    vir_energy,
    occ_count,
    vir_count,
    offset,
    a_half,
    b_half,
    b_other,
    b_mine,
    cand,
    a_turned,
    b_turned,
    base,
    keep,
    halves,
    total,
    landed,
    summed,
    parts,
    off_vectors,
    off_scalars,
    in_sems,
    z_send,
    z_recv,
    a_send,
    a_recv,
    cand_send,
    cand_recv,
    cand_pass,
    b_send,
    b_recv,
    b_share,
    relay_recv,
    off_sems,
    sum_send,
    sum_recv,
    part_send,
    part_recv,
):
    rows = blocks.shape[1]
    steps, padded, vir = a_half.shape
    aux_rows = vir // 4
    chips = frag_total // 2
    grid_rows = frag_total // ROW_FRAGS

    frag = lax.axis_index("frag")
    aux = lax.axis_index("aux")
    core = lax.rem(frag, 2)
    chip = frag // 2
    row = frag // ROW_FRAGS
    up = lax.rem(chip + 1, chips)
    down = lax.rem(chip + chips - 1, chips)
    sibling = chip * 2 + 1 - core
    next_row = lax.rem(frag + ROW_FRAGS, frag_total)
    last_row = lax.rem(frag + frag_total - ROW_FRAGS, frag_total)

    pair, q_half, mate, outer = place_in_ring(aux, row)
    far = lax.rem(aux + 2, 4)
    member = core == pair
    stranger = core != pair
    relay_pair, _, relay_to, _ = place_in_ring(aux, lax.rem(row + grid_rows - 1, grid_rows))
    relays = core == relay_pair

    ins = [
        pltpu.make_async_copy(there, here, in_sems.at[n])
        for n, (there, here) in enumerate(
            (
                (offset_in, offset),
                (occ_energy_in, occ_energy),
                (vir_energy_in, vir_energy),
                (occ_count_in, occ_count),
                (vir_count_in, vir_count),
            )
        )
    ]
    for copy in ins:
        copy.start()

    barrier = pltpu.get_barrier_semaphore()
    greeted = [(sibling, aux)]
    greeted += [(chip * 2 + n, other) for other in (mate, outer, far) for n in range(2)]
    greeted += [(there * 2 + n, aux) for there in (up, down) for n in range(2)]
    greeted += [(next_row, aux), (next_row, mate), (last_row, aux), (last_row, relay_to)]
    for there, other in greeted:
        pl.semaphore_signal(barrier, inc=1, device_id={"frag": there, "aux": other}, device_id_type=MESH)
    pl.semaphore_wait(barrier, len(greeted))

    first_rows = -(-rows // 32) * 16

    def own(s):
        return pl.ds(0, first_rows) if s.half == 0 else pl.ds(first_rows, rows - first_rows)

    def rows_of(who, s):
        here = own(s)
        return pl.ds(pl.multiple_of(who * rows + here.start, 16), here.size)

    def two_cols(s):
        return pl.ds(pl.multiple_of(s * 2 * vir, 128), 2 * vir)

    def z_copy(s):
        return to_device(
            blocks.at[0, own(s), two_cols(s.step)], a_stage.at[s.step, own(s)], z_send.at[s.step, s.half], z_recv.at[s.step, s.half], up * 2 + 1, aux
        )

    def cand_copy(s, slot, n, there):
        src = blocks.at[0, own(s), two_cols(s.step)]
        if there is None:
            return pltpu.make_async_copy(src, cand.at[slot, s.step, own(s)], cand_recv.at[slot, s.step, s.half])
        return to_device(src, cand.at[slot, s.step, own(s)], cand_send.at[n, s.step, s.half], cand_recv.at[slot, s.step, s.half], there, aux)

    def cand_forward(s):
        return to_device(cand.at[2, s.step, own(s)], cand.at[1, s.step, own(s)], cand_pass.at[s.step, s.half], cand_recv.at[1, s.step, s.half], sibling, aux)

    def z_up(s):
        @pl.when(core == 1)
        def _():
            z_copy(s).start()

    def z_down(s):
        @pl.when(core == 0)
        def _():
            cand_copy(s, 2, 1, down * 2 + 1).start()
            cand_copy(s, 0, 0, sibling).start()

        @pl.when(core == 1)
        def _():
            cand_copy(s, 2, 1, down * 2).start()
            cand_copy(s, 0, 0, sibling).start()
            cand_copy(s, 1, 0, None).start()

    def a_source(s, core_is, part):
        if core_is == 0:
            return blocks.at[0, own(s), pl.ds(pl.multiple_of(s.step * 2 * vir + part * vir, 128), vir)]
        return a_stage.at[s.step, own(s), pl.ds(part * vir, vir)]

    def a_own(s, core_is):
        return pltpu.make_async_copy(
            a_source(s, core_is, core_is), a_half.at[s.step, rows_of(aux, s)], a_recv.at[0, s.step, s.half]
        )

    def a_copy(s, core_is, part, kind):
        there, other = {0: (sibling, aux), 1: (chip * 2 + part, mate), 2: (chip * 2 + part, outer)}[kind]
        n = 0 if kind == 0 else 1 + part
        return to_device(
            a_source(s, core_is, part),
            a_half.at[s.step, rows_of(aux, s)],
            a_send.at[n, s.step, s.half],
            a_recv.at[kind, s.step, s.half],
            there,
            other,
        )

    def a_forward(s):
        here = a_half.at[s.step, rows_of(outer, s)]
        return to_device(here, here, a_send.at[3, s.step, s.half], a_recv.at[3, s.step, s.half], frag, mate)

    def a_landing(s, kind, who):
        here = a_half.at[s.step, rows_of(who, s)]
        return to_device(here, here, a_send.at[3, s.step, s.half], a_recv.at[kind, s.step, s.half], frag, mate)

    def begin_a(s):
        for core_is in range(2):
            @pl.when(core == core_is)
            def _():
                if core_is == 1:
                    z_copy(s).wait_recv()

                @pl.when(member)
                def _():
                    a_copy(s, core_is, 0, 1).start()
                    a_copy(s, core_is, 1, 1).start()
                    a_copy(s, core_is, 1 - core_is, 0).start()
                    a_own(s, core_is).start()

                @pl.when(stranger)
                def _():
                    a_copy(s, core_is, 0, 2).start()
                    a_copy(s, core_is, 1, 2).start()

    def b_round(s):
        return to_device(b_other.at[s.step, own(s)], relay.at[s.step, own(s)], b_send.at[0, s.step, s.half], relay_recv.at[s.step, s.half], next_row, aux)

    def b_relay(s):
        return to_device(
            relay.at[s.step, own(s)], b_half.at[s.step, rows_of(aux, s)], b_send.at[2, s.step, s.half], b_recv.at[1, s.step, s.half], last_row, relay_to
        )

    def b_outer(s):
        return to_device(
            b_other.at[s.step, own(s)], b_half.at[s.step, rows_of(aux, s)], b_send.at[0, s.step, s.half], b_recv.at[2, s.step, s.half], frag, outer
        )

    def b_through(s):
        return to_device(b_mine.at[s.step, own(s)], transit.at[s.step, own(s)], b_send.at[1, s.step, s.half], b_recv.at[0, s.step, s.half], frag, outer)

    def b_forward(s):
        return to_device(
            transit.at[s.step, own(s)], b_half.at[s.step, rows_of(outer, s)], b_send.at[1, s.step, s.half], b_recv.at[3, s.step, s.half], frag, mate
        )

    def b_landing(s, kind, who):
        here = b_half.at[s.step, rows_of(who, s)]
        return to_device(here, here, b_share.at[kind, s.step, s.half], b_recv.at[kind, s.step, s.half], sibling, aux)

    def chosen(s, which):
        cols = pl.ds(pl.multiple_of(which * vir, 128), vir)
        one, two, three = (cand[n, s.step, own(s), cols] for n in range(3))
        chosen_at = off_scalars[0, 0, 0]
        return jnp.where(chosen_at == 1, one, jnp.where(chosen_at == 2, two, three))

    def begin_b(s):
        @pl.when(core == 1)
        def _():
            cand_copy(s, 2, 1, down * 2).wait_recv()
            cand_forward(s).start()
            cand_copy(s, 0, 0, sibling).wait_recv()
            cand_copy(s, 1, 0, None).wait()

        @pl.when(core == 0)
        def _():
            cand_copy(s, 0, 0, sibling).wait_recv()
            cand_copy(s, 2, 1, down * 2 + 1).wait_recv()
            cand_forward(s).wait_recv()

        b_other[s.step, own(s), :] = chosen(s, 1 - q_half)

        @pl.when(member)
        def _():
            b_round(s).start()
            b_half[s.step, rows_of(aux, s), :] = chosen(s, q_half)
            b_landing(s, 0, aux).start()

        @pl.when(stranger)
        def _():
            b_outer(s).start()
            b_mine[s.step, own(s), :] = chosen(s, q_half)
            b_through(s).start()

    def pass_a(s):
        a_landing(s, 2, outer).wait_recv()
        a_forward(s).start()

    def pass_b(s):
        @pl.when(member)
        def _():
            b_through(s).wait_recv()
            b_forward(s).start()

        @pl.when(relays)
        def _():
            b_round(s).wait_recv()
            b_relay(s).start()

    def gather_a(s):
        @pl.when(member)
        def _():
            for core_is in range(2):
                @pl.when(core == core_is)
                def _():
                    a_own(s, core_is).wait()

        @pl.when(stranger)
        def _():
            a_landing(s, 0, aux).wait_recv()

        a_landing(s, 1, mate).wait_recv()
        a_landing(s, 3, far).wait_recv()

    def gather_b(s):
        @pl.when(member)
        def _():
            for kind, who in ((2, outer), (1, mate), (3, far)):
                b_landing(s, kind, who).wait_recv()
                b_landing(s, kind, who).start()

        @pl.when(stranger)
        def _():
            for kind, who in ((0, aux), (2, outer), (1, mate), (3, far)):
                b_landing(s, kind, who).wait_recv()

    ins[0].wait()

    def off_copy(n):
        if n == 0:
            return to_device(
                off_vectors.at[0], off_vectors.at[1], off_sems.at[0], off_sems.at[1], up * 2 + 1, aux
            )
        return to_device(off_vectors.at[1], off_vectors.at[2], off_sems.at[2], off_sems.at[3], sibling, aux)

    def off_read(n):
        return pltpu.make_async_copy(off_vectors.at[n], off_scalars.at[n - 1], off_sems.at[3 + n])

    own_offset = jnp.full(off_vectors.shape[1:], offset[0], jnp.int32)

    @pl.when(core == 0)
    def _():
        off_vectors[1] = own_offset

    @pl.when(core == 1)
    def _():
        off_vectors[0] = own_offset
        off_copy(0).start()

    def know_offsets():
        @pl.when(core == 1)
        def _():
            off_copy(0).wait()

        @pl.when(member)
        def _():
            off_copy(1).start()
            off_vectors[2] = off_vectors[1]

        off_read(1).start()
        off_read(1).wait()

    stages = {
        "z_up": z_up,
        "z_down": z_down,
        "a": begin_a,
        "b": begin_b,
        "pass_a": pass_a,
        "pass_b": pass_b,
        "gather_a": gather_a,
        "gather_b": gather_b,
    }
    for name, n in START:
        if (name, n) == ("b", 0):
            know_offsets()
        stages[name](Part(n // 2, n % 2))

    @pl.when(member)
    def _():
        off_copy(1).wait_send()

    @pl.when(stranger)
    def _():
        off_copy(1).wait_recv()

    off_read(2).start()
    if padded > 4 * rows:
        for half in (a_half, b_half):
            @pl.loop(0, steps)
            def _(s):
                half[s, 4 * rows :, :] = jnp.zeros((padded - 4 * rows, vir), jnp.bfloat16)

    off_read(2).wait()
    distance = off_scalars[1, 0, 0]
    for copy in ins[1:]:
        copy.wait()
    leader = jnp.where(pair == 0, chip * 2, lax.rem(chip * 2 + frag_total - 1, frag_total))
    partner = jnp.minimum(leader + distance, frag_total - 1)
    valid = leader + distance < frag_total
    leader_occ = occ_count[leader]
    partner_occ = occ_count[partner]
    leader_vir = vir_count[leader]
    partner_vir = vir_count[partner]

    leader_levels = vir_energy[pl.ds(leader, 1), :]
    partner_levels = vir_energy[pl.ds(partner, 1), :]
    row_ids = lax.broadcasted_iota(jnp.int32, (vir, vir), 0)
    col_ids = lax.broadcasted_iota(jnp.int32, (vir, vir), 1)
    base[0] = -leader_levels - jnp.broadcast_to(partner_levels, (vir, vir)).T
    base[1] = -partner_levels - jnp.broadcast_to(leader_levels, (vir, vir)).T
    keep[0] = jnp.where((row_ids < partner_vir) & (col_ids < leader_vir), 1.0, 0.0)
    keep[1] = jnp.where((row_ids < leader_vir) & (col_ids < partner_vir), 1.0, 0.0)
    total[...] = jnp.zeros(total.shape, jnp.float32)

    def amplitudes(i, j, way):
        lead_occ = 2 * i + core
        part_occ = 2 * j + q_half
        ok = jnp.logical_and(valid, jnp.logical_and(lead_occ < leader_occ, part_occ < partner_occ))
        level = occ_energy[lead_occ, leader] + occ_energy[part_occ, partner]
        turned, straight = (b_turned, a_half.at[i]) if way == 0 else (a_turned, b_half.at[j])
        integrals = jnp.dot(turned[...], straight[...], preferred_element_type=jnp.float32)
        amplitude = integrals * (keep[way] * jnp.where(ok, 1.0, 0.0)) / (base[way] + level)
        energy = amplitude * integrals
        total[0, 2 * aux_rows :, :] += energy.reshape(vir // 8, 8, vir).sum(0)
        return amplitude.astype(jnp.bfloat16)

    def squares(rounded, way):
        of_cols, of_rows = 0.0, 0.0
        for each in rounded:
            of_cols += lax.dot_general(each, each, (((0,), (0,)), ((), ())), preferred_element_type=jnp.float32)
            of_rows += lax.dot_general(each, each, (((1,), (1,)), ((), ())), preferred_element_type=jnp.float32)
        first, second = (of_cols, of_rows) if way == 0 else (of_rows, of_cols)
        for n in range(4):
            piece = slice(n * aux_rows, (n + 1) * aux_rows)
            total[n, :aux_rows, :] += first[piece]
            total[n, aux_rows : 2 * aux_rows, :] += second[piece]

    def tiles(count, way, place):
        def two(n):
            for m in range(2):
                halves[m] = amplitudes(*place(2 * n + m), way)

        @pl.when(count > 1)
        def _():
            two(0)

            @pl.loop(1, count // 2)
            def _(n):
                squares([halves[m] for m in range(2)], way)
                two(n)

            squares([halves[m] for m in range(2)], way)

        @pl.when(lax.rem(count, 2) == 1)
        def _():
            squares([amplitudes(*place(count - 1), way)], way)

    def columns(s):
        for at in range(0, padded, BLOCK):
            b_turned[:, at : at + BLOCK] = b_half[s, at : at + BLOCK, :].T
        tiles(jnp.minimum(s + 2, steps), 0, lambda n: (n, s))

    def across(s):
        @pl.when(s + 1 < steps)
        def _():
            for at in range(0, padded, BLOCK):
                a_turned[:, at : at + BLOCK] = a_half[s + 1, at : at + BLOCK, :].T
            tiles(s, 1, lambda n: (s + 1, n))

    stages["columns"] = columns
    stages["across"] = across

    def drain(step):
        for s in (Part(step, 0), Part(step, 1)):
            cand_copy(s, 0, 0, sibling).wait_send()
            cand_copy(s, 2, 1, sibling).wait_send()
            a_forward(s).wait_send()
            for core_is in range(2):
                @pl.when(core == core_is)
                def _():
                    a_copy(s, core_is, 0, 1).wait_send()
                    a_copy(s, core_is, 1, 1).wait_send()

                    @pl.when(member)
                    def _():
                        a_copy(s, core_is, 1 - core_is, 0).wait_send()

            @pl.when(core == 1)
            def _():
                z_copy(s).wait_send()
                cand_forward(s).wait_send()

            @pl.when(member)
            def _():
                for kind, who_is in enumerate((aux, mate, outer, far)):
                    b_landing(s, kind, who_is).wait_send()

            b_round(s).wait_send()
            b_through(s).wait_send()

            @pl.when(relays)
            def _():
                b_relay(s).wait_send()

    @pl.loop(0, steps)
    def _(s):
        for half in range(2):
            for name, lead in ORDER:
                part = Part(s + (half + lead) // 2, (half + lead) % 2)
                if (name, half) == ("gather_b", 0):
                    @pl.when(s >= KEPT)
                    def _():
                        drain(s - KEPT)

                if name in ("columns", "across"):
                    if part.half != (name == "columns"):
                        continue
                    part = part.step

                @pl.when(s + (half + lead) // 2 < steps)
                def _():
                    stages[name](part)

    for n in range(1, 4):
        total[n, 2 * aux_rows :, :] = total[0, 2 * aux_rows :, :]
    who = q_half * 2 + core

    def sum_copy(n):
        column = lax.rem(aux + n, 4)
        there = sibling if n == 0 else chip * 2 + pair
        return to_device(total.at[column], landed.at[who], sum_send.at[n], sum_recv.at[who], there, column)

    def sum_landing(n):
        return to_device(landed.at[n], landed.at[n], sum_send.at[0], sum_recv.at[n], sibling, aux)

    for n in (2, 1, 3):
        sum_copy(n).start()

    @pl.when(stranger)
    def _():
        sum_copy(0).start()

    @pl.when(member)
    def _():
        landed[who] = total[aux]

    @pl.loop(steps - KEPT, steps)
    def _(step):
        drain(step)

    for n in range(1, 4):
        sum_copy(n).wait_send()

    @pl.when(stranger)
    def _():
        sum_copy(0).wait_send()

    for n in range(4):
        @pl.when(jnp.logical_or(stranger, who != n))
        def _():
            sum_landing(n).wait_recv()

    own_distance = off_scalars[0, 0, 0]
    sums = landed[0] + landed[1] + landed[2] + landed[3]
    summed[0, :aux_rows, :] = sums[:aux_rows]
    summed[0, aux_rows:, :] = sums[2 * aux_rows :]
    for n in range(1, 4):
        summed[n, :aux_rows, :] = jnp.where(own_distance == n, sums[aux_rows : 2 * aux_rows], 0.0)

    def part_copy(n):
        there = (
            down * 2 + 1,
            sibling,
            up * 2,
            jnp.where(core == 0, up * 2 + 1, up * 2),
        )[n]
        if n == 0:
            src, dst = summed.at[0], parts.at[0]
        else:
            src, dst = summed.at[n, pl.ds(0, aux_rows)], parts.at[n, pl.ds(0, aux_rows)]
        return to_device(src, dst, part_send.at[n], part_recv.at[n], there, aux)

    for n in (0, 2):
        stays = core == n // 2

        @pl.when(core != n // 2)
        def _():
            part_copy(n).start()

        @pl.when(stays)
        def _():
            parts[n] = summed[n]

    for n in (1, 3):
        part_copy(n).start()
    for n in (1, 3):
        part_copy(n).wait()
    for n in (0, 2):
        stays = core == n // 2

        @pl.when(core != n // 2)
        def _():
            part_copy(n).wait()

    density_out[0] = (
        parts[0, :aux_rows, :] + parts[1, :aux_rows, :] + parts[2, :aux_rows, :] + parts[3, :aux_rows, :]
    )
    energy_out[0] = jnp.sum(parts[0, aux_rows:, :])


def on_device(blocks, occ_energy, vir_energy, occ_count, vir_count, partner_offset):
    frag_total, occ = occ_energy.shape
    vir = vir_energy.shape[1]
    rows = blocks.shape[1]
    steps = occ // 2
    padded = -(-4 * rows // BLOCK) * BLOCK
    aux_rows = vir // 4
    vmem = pl.BlockSpec(memory_space=pltpu.VMEM)
    smem = pl.BlockSpec(memory_space=pltpu.SMEM)
    anywhere = pl.BlockSpec(memory_space=pl.ANY)
    dma = pltpu.SemaphoreType.DMA
    results = pl.pallas_call(
        functools.partial(kernel, frag_total),
        out_shape=(
            jax.ShapeDtypeStruct((1,), jnp.float32),
            jax.ShapeDtypeStruct((1, aux_rows, vir), jnp.float32),
            jax.ShapeDtypeStruct((steps, rows, 2 * vir), jnp.bfloat16),
            jax.ShapeDtypeStruct((steps, rows, vir), jnp.bfloat16),
            jax.ShapeDtypeStruct((steps, rows, vir), jnp.bfloat16),
        ),
        in_specs=[anywhere] * 6,
        out_specs=(smem, vmem, anywhere, anywhere, anywhere),
        scratch_shapes=[
            pltpu.SMEM((occ, frag_total), jnp.float32),
            pltpu.VMEM((frag_total, vir), jnp.float32),
            pltpu.SMEM((frag_total,), jnp.int32),
            pltpu.SMEM((frag_total,), jnp.int32),
            pltpu.SMEM((1,), jnp.int32),
            pltpu.VMEM((steps, padded, vir), jnp.bfloat16),
            pltpu.VMEM((steps, padded, vir), jnp.bfloat16),
            pltpu.VMEM((steps, rows, vir), jnp.bfloat16),
            pltpu.VMEM((steps, rows, vir), jnp.bfloat16),
            pltpu.VMEM((3, steps, rows, 2 * vir), jnp.bfloat16),
            pltpu.VMEM((vir, padded), jnp.bfloat16),
            pltpu.VMEM((vir, padded), jnp.bfloat16),
            pltpu.VMEM((2, vir, vir), jnp.float32),
            pltpu.VMEM((2, vir, vir), jnp.float32),
            pltpu.VMEM((2, vir, vir), jnp.bfloat16),
            pltpu.VMEM((4, 2 * aux_rows + 8, vir), jnp.float32),
            pltpu.VMEM((4, 2 * aux_rows + 8, vir), jnp.float32),
            pltpu.VMEM((4, aux_rows + 8, vir), jnp.float32),
            pltpu.VMEM((4, aux_rows + 8, vir), jnp.float32),
            pltpu.VMEM((3, 8, 128), jnp.int32),
            pltpu.SMEM((2, 8, 128), jnp.int32),
            dma((5,)),
            dma((steps, 2)),
            dma((steps, 2)),
            dma((4, steps, 2)),
            dma((4, steps, 2)),
            dma((2, steps, 2)),
            dma((3, steps, 2)),
            dma((steps, 2)),
            dma((3, steps, 2)),
            dma((4, steps, 2)),
            dma((4, steps, 2)),
            dma((steps, 2)),
            dma((6,)),
            dma((4,)),
            dma((4,)),
            dma((4,)),
            dma((4,)),
        ],
        compiler_params=pltpu.CompilerParams(
            collective_id=0, has_side_effects=True, vmem_limit_bytes=60 * 1024 * 1024
        ),
        cost_estimate=pl.CostEstimate(
            flops=2 * 4 * rows * (occ * vir // 2) ** 2, bytes_accessed=2 * rows * occ * vir, transcendentals=0
        ),
        name="pair_terms",
    )(blocks, occ_energy.T, vir_energy, occ_count, vir_count, partner_offset)
    return results[0], results[1]


def solution(mesh):
    placed = (P("frag", "aux", None), P(), P(), P(), P(), P("frag"))
    return jax.shard_map(
        on_device,
        mesh=mesh,
        in_specs=placed,
        out_specs=(P("frag"), P("frag", "aux", None)),
        check_vma=False,
    )
```
